32 devices in a mesh: tx: 4 (over y, core), ty: 8 (over z, x).
Axes of the slice: x: 2, y: 2, z: 4, core: 2. Of those that a mesh axis runs over, the one named last changes fastest.
Arguments:
- increment: float32 [13, 2, 256, 512], P(None, None, 'ty', 'tx'), may hold values from -6 to 6
- blocks: bfloat16 [13, 13, 2, 256, 512], P(None, None, None, 'ty', 'tx'), may hold values from -1.75 to 1.75
- face_weights: float32 [3, 2, 256, 512], P(None, None, 'ty', 'tx'), may hold values from 0.25 to 2
- connected: int32 [3, 2, 256, 512], P(None, None, 'ty', 'tx'), may hold values 0 or 1
- overland_decay: float32 [13, 512, 256], P(None, 'tx', 'ty'), may hold values from 0.4 to 1
- river_cell: int32 [4, 8, 256], P('tx', 'ty'), may hold values from 0 to 4095
- river_reach: int32 [4, 8, 256], P('tx', 'ty'), may hold values from 0 to 255
- river_count: int32 [4, 8], P('tx', 'ty'), may hold values from 64 to 256, as said below
- inflow: float32 [4, 8, 256], P('tx', 'ty'), may hold values from -6 to 6
- outflow: float32 [4, 8, 256], P('tx', 'ty'), may hold values from -3 to 3
- storage: float32 [8, 256], P('ty', 'tx'), may hold values from 1 to 8
Outputs:
- jacobian_product: float32 [13, 2, 256, 512], P(None, None, 'ty', 'tx')
The draws below stay inside these ranges and needn't reach their ends.
Inputs may be any that keep to these rules, and one draw needn't show every extreme that they name: Each device's live river slots are its first river_count slots; some device fills all 256.
All inputs are finite; a program needn't handle non-finite values. No bound on the sum of `connected` on one device may be relied on, other than what follows from the above.
Results may differ from the reference program's by a relative error of at most 0.0003.
Values sent between devices are 32-bit elements; how exact they have to be, the bound alone decides.
No kernel may reach another device: no remote copies, remote signals or barrier semaphores. Data moves between devices by JAX's collectives and lax.ppermute only.
A program may use at most 128 MiB of HBM per device.

```python
import math
import jax
import jax.numpy as jnp
import numpy as np
from jax import lax

CELL_UNKNOWNS = 13
L = 2
CX = 128
CY = 32
RIV = 256
GRID_COLUMNS_X = 512
NY = 256
NR = 256
N_TX = 4
N_TY = 8


def draw_overland_decay(key, part):
    random_keys = jax.random.split(key, 6)
    slow_share = 0.5
    slow = jax.random.bernoulli(random_keys[0], slow_share, (CELL_UNKNOWNS, 1, GRID_COLUMNS_X))
    spread = jax.random.uniform(random_keys[1], (CELL_UNKNOWNS, 1, GRID_COLUMNS_X), jnp.float32, 0.2, 2.0)
    rough = jax.random.uniform(random_keys[2], (CELL_UNKNOWNS, NY, GRID_COLUMNS_X), jnp.float32, 0.5, 1.5)
    memory = jax.random.uniform(random_keys[3], (CELL_UNKNOWNS, 1, GRID_COLUMNS_X), jnp.float32, 30.0, 50.0)
    slow_rate = spread * rough / NY
    fast_rate = rough / memory
    multiplier = 1.0 - jnp.where(slow, slow_rate, fast_rate)
    places = jax.random.randint(random_keys[4], (4,), 0, NY)
    matched_entry = jnp.any(jnp.arange(NY, dtype=jnp.int32)[:, None] == places[None, :], axis=1)
    sudden_pulse = jax.random.uniform(random_keys[5], (CELL_UNKNOWNS, 1, GRID_COLUMNS_X), jnp.float32, 0.5, 0.8)
    multiplier = jnp.where(matched_entry[None, :, None], multiplier * sudden_pulse, multiplier)
    return jnp.swapaxes(multiplier, 1, 2).astype(jnp.float32)


def draw_river_count(key, part):
    random_keys = jax.random.split(key, 2)
    counts = jax.random.randint(random_keys[0], (N_TX, N_TY), RIV // 4, RIV + 1)
    chosen = jax.random.randint(random_keys[1], (), 0, N_TX * N_TY)
    flat = jnp.arange(N_TX * N_TY, dtype=jnp.int32).reshape(N_TX, N_TY)
    return jnp.where(flat == chosen, RIV, counts).astype(jnp.int32)


def with_ends(array, own_key, smallest, largest):
    place = [jax.random.randint(jax.random.fold_in(own_key, axis), (), 0, length) for axis, length in enumerate(array.shape)]
    longest = array.shape.index(max(array.shape))
    neighbour = place[:longest] + [(place[longest] + 1) % array.shape[longest]] + place[longest + 1:]
    return array.at[tuple(place)].set(smallest).at[tuple(neighbour)].set(largest)


def block_levels(stream_key, extent, cuts, smallest, largest):
    factor_of = 1.0
    for dim, parts in cuts:
        steps = jax.random.uniform(jax.random.fold_in(jax.random.fold_in(stream_key, 6), dim), (parts,), jnp.float32, smallest / len(cuts), largest / len(cuts))
        factor_of = factor_of * jnp.repeat(jnp.exp(steps), extent[dim] // parts).reshape((-1,) + (1,) * (len(extent) - 1 - dim))
    return factor_of


def cumulative_ranks(count, slope):
    portions = [(1 << 20) // math.isqrt(rank ** slope) + 1 for rank in range(1, count + 1)]
    scale = 1 + sum(portions) // (1 << 30)
    return np.cumsum(np.array([max(1, weight // scale) for weight in portions]))


def ranked_ids(stream_key, shape, count, skew):
    table = cumulative_ranks(count, skew)
    pick = jax.random.randint(jax.random.fold_in(stream_key, 1), shape, 0, int(table[count - 1]))
    standing = jnp.searchsorted(jnp.asarray(table, jnp.int32), pick, side="right")
    return jax.random.permutation(jax.random.fold_in(stream_key, 2), count)[standing].astype(jnp.int32)


def noise(own_key, extent, deviation, bound, cuts=(), kind=jnp.bfloat16):
    drawn = jax.random.normal(own_key, extent, jnp.float32) * deviation
    if len(cuts) > 0:
        drawn = block_levels(own_key, extent, cuts, -0.22, 0.18) * drawn
    return jnp.clip(drawn, min=-bound, max=bound).astype(kind)


def setup_inputs(seed: int = 0) -> dict:
    arg_keys = jax.random.split(jax.random.key(seed), 12)
    increment = noise(arg_keys[0], (CELL_UNKNOWNS, L, NY, GRID_COLUMNS_X), 1.0, 6.0, ((2, 8), (3, 4)), jnp.float32)
    blocks = noise(arg_keys[1], (CELL_UNKNOWNS, CELL_UNKNOWNS, L, NY, GRID_COLUMNS_X), CELL_UNKNOWNS ** -0.5, 1.75, ((3, 8), (4, 4)))
    face_weights = jnp.clip(0.25 + 1.75 * jax.random.uniform(arg_keys[2], (3, L, NY, GRID_COLUMNS_X), jnp.float32) ** block_levels(arg_keys[2], (3, L, NY, GRID_COLUMNS_X), ((2, 8), (3, 4)), -0.2, 0.2), 0.25, 2.0)
    connected = with_ends((jax.random.randint(arg_keys[3], (3, L, NY, GRID_COLUMNS_X), 0, 4) < 3).astype(jnp.int32), jax.random.fold_in(arg_keys[3], 1), 0, 1)
    overland_decay = draw_overland_decay(jax.random.fold_in(arg_keys[11], 71), 0)
    river_cell = with_ends(jax.random.randint(arg_keys[5], (N_TX, N_TY, RIV), 0, CY * CX), jax.random.fold_in(arg_keys[5], 1), 0, (CY * CX) - 1).astype(jnp.int32)
    river_reach = with_ends(ranked_ids(arg_keys[6], (N_TX, N_TY, RIV), NR, 2), jax.random.fold_in(arg_keys[6], 3), 0, NR - 1).astype(jnp.int32)
    river_count = draw_river_count(jax.random.fold_in(arg_keys[11], 71), 0)
    inflow = noise(arg_keys[8], (N_TX, N_TY, RIV), 1.0, 6.0, ((0, 4), (1, 8)), jnp.float32)
    outflow = noise(arg_keys[9], (N_TX, N_TY, RIV), 0.5, 3.0, ((0, 4), (1, 8)), jnp.float32)
    storage = jnp.clip(jnp.exp(math.log(8.0) - 2.0794415 * jax.random.uniform(arg_keys[10], (N_TY, NR), jnp.float32) ** block_levels(arg_keys[10], (N_TY, NR), ((0, 8), (1, 4)), -0.2, 0.2)), 1.0, 8.0)
    return {"increment": increment, "blocks": blocks, "face_weights": face_weights, "connected": connected, "overland_decay": overland_decay, "river_cell": river_cell, "river_reach": river_reach, "river_count": river_count, "inflow": inflow, "outflow": outflow, "storage": storage}


def combine_decay(prior_result, later):
    return (prior_result[0] * later[0], prior_result[1] * later[0] + later[1])


def block_terms(increment, blocks):
    result = jnp.zeros(increment.shape, jnp.float32)
    for source in range(increment.shape[0]):
        result = result + blocks[:, source].astype(jnp.float32) * increment[source][None]
    return result


def lateral_terms(padded, effective, unknowns):
    centre = padded[:unknowns, :, 1:-1, 1:-1]
    plus_x = padded[:unknowns, :, 1:-1, 2:]
    minus_x = padded[:unknowns, :, 1:-1, :-2]
    left_face = padded[unknowns, :, 1:-1, :-2]
    plus_y = padded[:unknowns, :, 2:, 1:-1]
    minus_y = padded[:unknowns, :, :-2, 1:-1]
    lower_face = padded[unknowns + 1, :, :-2, 1:-1]
    flux = effective[0] * (centre - plus_x) + left_face * (centre - minus_x)
    flux = flux + effective[1] * (centre - plus_y) + lower_face * (centre - minus_y)
    return flux


def vertical_terms(increment, interface_depth):
    padded = jnp.pad(increment, ((0, 0), (1, 1), (0, 0), (0, 0)))
    above_face = jnp.pad(interface_depth, ((1, 0), (0, 0), (0, 0)))[:-1]
    return interface_depth * (increment - padded[:, 2:]) + above_face * (increment - padded[:, :-2])


def reference(increment, blocks, face_weights, connected, overland_decay, river_cell, river_reach, river_count, inflow, outflow, storage):
    unknowns = increment.shape[0]
    effective = face_weights * connected.astype(jnp.float32)
    stacked = jnp.concatenate([increment, effective[:2]], 0)
    padded = jnp.pad(stacked, ((0, 0), (0, 0), (1, 1), (1, 1)))
    total = block_terms(increment, blocks)
    total = total + lateral_terms(padded, effective, unknowns)
    total = total + vertical_terms(increment, effective[2])
    decay_yx = jnp.swapaxes(overland_decay, 1, 2)
    factors, routed = lax.associative_scan(combine_decay, (decay_yx, increment[:, 0]), axis=1)
    total = total.at[:, 0].add(0.1 * routed)
    index_x = jnp.arange(N_TX, dtype=jnp.int32)[:, None, None]
    index_y = jnp.arange(N_TY, dtype=jnp.int32)[None, :, None]
    global_y = index_y * CY + river_cell // CX
    global_x = index_x * CX + river_cell % CX
    values = increment[0, 0][global_y, global_x]
    live = (jnp.arange(RIV, dtype=jnp.int32)[None, None, :] < river_count[:, :, None]).astype(jnp.float32)
    random_keys = index_y * NR + river_reach
    totals = jax.ops.segment_sum((inflow * values * live).reshape(-1), random_keys.reshape(-1), num_segments=N_TY * NR)
    sections = totals / storage.reshape(-1)
    back = outflow * sections[random_keys] * live
    flat_cells = (global_y * GRID_COLUMNS_X + global_x).reshape(-1)
    river_add = jax.ops.segment_sum(back.reshape(-1), flat_cells, num_segments=NY * GRID_COLUMNS_X).reshape(NY, GRID_COLUMNS_X)
    total = total.at[0, 0].add(river_add)
    return total
```

```python
import functools
import jax
import jax.numpy as jnp
from jax import lax
from jax.experimental import pallas as pl
from jax.experimental.pallas import tpu as pltpu
from jax.sharding import PartitionSpec as P

F32 = jnp.float32
BF16 = jnp.bfloat16
LANES = 128


def log2(n):
    return n.bit_length() - 1


def swap(x, axis, k):
    n = lax.axis_size(axis)
    mask = (2 << k) - 1
    return lax.ppermute(x, axis, [(i, i ^ mask) for i in range(n)])


def bit_of(axis, k):
    return (lax.axis_index(axis) >> k) & 1


def split3(x):
    hi = x.astype(BF16).astype(F32)
    rest = x - hi
    mid = rest.astype(BF16).astype(F32)
    return hi, mid, rest - mid


def stack3(row, height):
    hi, mid, lo = split3(row)
    at = lax.broadcasted_iota(jnp.int32, (height, row.shape[1]), 0)
    zero = jnp.zeros((height, row.shape[1]), F32)
    out = jnp.where(at == 0, hi, jnp.where(at == 1, mid, jnp.where(at == 2, lo, zero)))
    return out.astype(BF16)


def hot(index_row, size, start=0):
    at = lax.broadcasted_iota(jnp.int32, (size, index_row.shape[1]), 0) + start
    return at == index_row


def send_kernel(
    inc_ref, dec_ref, fw_ref, con_ref, cell_ref, reach_ref, count_ref, inflow_ref, storage_ref,
    ysend_ref, rims_ref, xsend_ref,
):
    unknowns, layers, rows, cols = inc_ref.shape
    cells = cell_ref[0]
    reaches = reach_ref[0]
    slots = cells.shape[1]
    shift = log2(cols)
    cell_y = cells >> shift
    cell_x = cells & (cols - 1)
    hi, mid, lo = split3(inc_ref[0, 0])
    parts = jnp.concatenate([hi, mid, lo], 0).astype(BF16)
    y_hot = hot(cell_y, rows).astype(F32)
    y_hot3 = jnp.concatenate([y_hot, y_hot, y_hot], 0).astype(BF16)
    picked = lax.dot_general(parts, y_hot3, (((0,), (0,)), ((), ())), preferred_element_type=F32)
    values = jnp.sum(jnp.where(hot(cell_x, cols), picked, 0.0), 0, keepdims=True)
    live = lax.broadcasted_iota(jnp.int32, (1, slots), 1) < count_ref[...]
    terms = stack3(jnp.where(live, inflow_ref[0] * values, 0.0), 16)
    reach_local = storage_ref.shape[1]
    x_index = lax.axis_index("tx")
    reach_rows = reach_local * lax.axis_size("tx") // LANES
    pad = (xsend_ref.shape[0] - rows) // 2
    stored = jnp.concatenate([storage_ref[...]] * (LANES // reach_local), 1)
    owner = lax.broadcasted_iota(jnp.int32, (1, LANES), 1)
    for c in range(reach_rows):
        r_hot = hot(reaches, LANES, c * LANES).astype(F32).astype(BF16)
        total = lax.dot_general(terms, r_hot, (((1,), (1,)), ((), ())), preferred_element_type=F32)
        xsend_ref[pl.ds(rows + c, 1), :] = jnp.sum(total, 0, keepdims=True)
        xsend_ref[pl.ds(rows + pad + c, 1), :] = jnp.where(
            (owner + c * LANES) // reach_local == x_index, stored, 0.0
        )
    if pad > reach_rows:
        xsend_ref[pl.ds(rows + reach_rows, pad - reach_rows), :] = jnp.zeros((pad - reach_rows, LANES), F32)
        xsend_ref[pl.ds(rows + pad + reach_rows, pad - reach_rows), :] = jnp.zeros((pad - reach_rows, LANES), F32)
    pair = lax.broadcasted_iota(jnp.int32, (rows, cols), 1) >> 1
    packed = jnp.zeros((rows, cols), F32)
    for p in range(unknowns * layers + layers):
        if p < unknowns * layers:
            plane = inc_ref[p // layers, p % layers]
        else:
            layer = p - unknowns * layers
            plane = fw_ref[0, layer] * con_ref[0, layer].astype(F32)
        packed = jnp.where(pair == p, pltpu.roll(plane, 2 * p + 1, 1), packed)
    xsend_ref[0:rows, :] = packed
    ysend_ref[...] = jnp.zeros(ysend_ref.shape, F32)
    rims_ref[...] = jnp.zeros(rims_ref.shape, F32)
    upper = bit_of("ty", 0) == 1
    for layer in range(layers):
        first = inc_ref[:, layer, 0, :]
        last = inc_ref[:, layer, rows - 1, :]
        rims_ref[0, layer, 0:unknowns] = first
        rims_ref[1, layer, 0:unknowns] = last
        ysend_ref[2 + layer, 0:unknowns] = jnp.where(upper, first, last)
        face = fw_ref[1, layer, rows - 1:rows, :] * con_ref[1, layer, rows - 1:rows, :].astype(F32)
        ysend_ref[layer, unknowns:unknowns + 1] = face
    product = dec_ref[:, 0, :]
    value = inc_ref[:, 0, 0, :]
    for y in range(1, rows):
        decay = dec_ref[:, y, :]
        product = product * decay
        value = value * decay + inc_ref[:, 0, y, :]
    ysend_ref[0, 0:unknowns] = product
    ysend_ref[1, 0:unknowns] = value


def prefix_step(k, received, prior):
    upper = bit_of("ty", k) == 1
    product = jnp.where(upper, prior[0] * received[0], prior[0])
    value = jnp.where(upper, prior[0] * received[1] + prior[1], prior[1])
    return product, value


def between_kernel(k, unknowns, sent_ref, got_ref, prior_ref, rims_ref, send_ref, next_ref):
    upper = bit_of("ty", k) == 1
    product, value = prefix_step(k, got_ref, prior_ref)
    next_ref[0] = product
    next_ref[1] = value
    keep = lax.broadcasted_iota(jnp.int32, sent_ref.shape[1:], 0) >= unknowns
    own_a, own_b, got_a, got_b = sent_ref[0], sent_ref[1], got_ref[0], got_ref[1]
    low_b = jnp.where(upper, got_b, own_b)
    up_a = jnp.where(upper, own_a, got_a)
    up_b = jnp.where(upper, own_b, got_b)
    send_ref[0] = jnp.where(keep, own_a, own_a * got_a)
    send_ref[1] = jnp.where(keep, own_b, up_a * low_b + up_b)
    later = bit_of("ty", k + 1) == 1
    for layer in range(rims_ref.shape[1]):
        send_ref[2 + layer] = jnp.where(later, rims_ref[0, layer], rims_ref[1, layer])


def from_neighbours(axis, received):
    index = lax.axis_index(axis)
    above = jnp.zeros(received[0].shape, F32)
    below = jnp.zeros(received[0].shape, F32)
    for k, buffer in enumerate(received):
        low = (1 << k) - 1
        full = (2 << k) - 1
        above = jnp.where((index & full) == low, buffer, above)
        below = jnp.where((index & full) == low + 1, buffer, below)
    return below, above


def local_kernel(
    x_rounds, reach_rows, inc_ref, blocks_ref, fw_ref, con_ref, dec_ref, cell_ref, reach_ref, count_ref, outflow_ref,
    sent_ref, *refs,
):
    received = refs[:x_rounds]
    out_ref, grown_ref = refs[x_rounds:]
    unknowns, layers, rows, cols = inc_ref.shape
    lane = lax.broadcasted_iota(jnp.int32, (rows, cols), 1)
    row = lax.broadcasted_iota(jnp.int32, (rows, cols), 0)
    slab = 16
    for layer in range(layers):
        for s in range(rows // slab):
            at = pl.ds(s * slab, slab)
            sources = [inc_ref[j, layer, at, :] for j in range(unknowns)]
            for i in range(unknowns):
                acc = blocks_ref[i, 0, layer, at, :].astype(F32) * sources[0]
                for j in range(1, unknowns):
                    acc = acc + blocks_ref[i, j, layer, at, :].astype(F32) * sources[j]
                out_ref[i, layer, at, :] = acc
    left, right = from_neighbours("tx", [r[0:rows, :] for r in received])
    rim = jnp.where(lane & 1 == 0, pltpu.roll(right, cols - 1, 1), pltpu.roll(left, 1, 1))
    planes = unknowns * layers
    face = [[fw_ref[d, l] * con_ref[d, l].astype(F32) for l in range(layers)] for d in range(3)]
    for layer in range(layers):
        face_x = face[0][layer]
        face_y = jnp.where(row == rows - 1, 0.0, face[1][layer])
        face_left = pltpu.roll(rim, (cols - 1 - 2 * (planes + layer)) % cols, 1)
        for u in range(unknowns):
            here = inc_ref[u, layer]
            p = u * layers + layer
            beside = pltpu.roll(rim, cols - 1 - 2 * p, 1)
            flow_x = face_x * (here - jnp.where(lane == cols - 1, beside, pltpu.roll(here, cols - 1, 1)))
            from_left = jnp.where(lane == 0, face_left * (beside - here), pltpu.roll(flow_x, 1, 1))
            flow_y = face_y * (here - pltpu.roll(here, rows - 1, 0))
            total = flow_x - from_left + (flow_y - pltpu.roll(flow_y, 1, 0))
            if layer + 1 < layers:
                total = total + face[2][layer] * (here - inc_ref[u, layer + 1])
            else:
                total = total + face[2][layer] * here
            if layer > 0:
                total = total + face[2][layer - 1] * (here - inc_ref[u, layer - 1])
            out_ref[u, layer] += total
    product = dec_ref[:, 0, :]
    value = inc_ref[:, 0, 0, :]
    grown_ref[:, 0, :] = 0.1 * product
    out_ref[:, 0, 0, :] += 0.1 * value
    for y in range(1, rows):
        decay = dec_ref[:, y, :]
        product = product * decay
        value = value * decay + inc_ref[:, 0, y, :]
        grown_ref[:, y, :] = 0.1 * product
        out_ref[:, 0, y, :] += 0.1 * value
    pad = (sent_ref.shape[0] - rows) // 2
    totals = sent_ref[rows:rows + pad, :] + received[-1][rows:rows + pad, :]
    storage = sent_ref[rows + pad:, :] + received[-1][rows + pad:, :]
    cells = cell_ref[0]
    reaches = reach_ref[0]
    slots = cells.shape[1]
    shift = log2(cols)
    picked = jnp.zeros((16, slots), F32)
    for c in range(reach_rows):
        section = stack3(totals[c:c + 1] / storage[c:c + 1], 16)
        r_hot = hot(reaches, LANES, c * LANES).astype(F32).astype(BF16)
        picked = picked + lax.dot_general(section, r_hot, (((1,), (0,)), ((), ())), preferred_element_type=F32)
    live = lax.broadcasted_iota(jnp.int32, (1, slots), 1) < count_ref[...]
    back = jnp.where(live, outflow_ref[0] * jnp.sum(picked, 0, keepdims=True), 0.0)
    y_hot = hot(cells >> shift, rows)
    spread = jnp.concatenate([jnp.where(y_hot, part, 0.0) for part in split3(back)], 0).astype(BF16)
    x_hot = hot(cells & (cols - 1), cols).astype(F32).astype(BF16)
    added = lax.dot_general(spread, x_hot, (((1,), (1,)), ((), ())), preferred_element_type=F32)
    out_ref[0, 0] += added[0:rows] + added[rows:2 * rows] + added[2 * rows:3 * rows]


def final_kernel(y_rounds, part_ref, grown_ref, inc_ref, fw_ref, con_ref, prior_ref, *refs):
    received = refs[:y_rounds]
    out_ref = refs[y_rounds]
    unknowns, layers, rows, cols = inc_ref.shape
    _, value = prefix_step(y_rounds - 1, received[-1], prior_ref)
    carry = value[0:unknowns]
    below, above = from_neighbours("ty", [r[...] for r in received])
    out_ref[...] = part_ref[...]
    for u in range(unknowns):
        out_ref[u, 0] += grown_ref[u] * carry[u:u + 1]
    for layer in range(layers):
        last = rows - 1
        top_face = fw_ref[1, layer, last:rows, :] * con_ref[1, layer, last:rows, :].astype(F32)
        low_face = below[layer, unknowns:unknowns + 1]
        first = inc_ref[:, layer, 0, :] - below[2 + layer, 0:unknowns]
        final = inc_ref[:, layer, last, :] - above[2 + layer, 0:unknowns]
        out_ref[:, layer, 0, :] += low_face * first
        out_ref[:, layer, last, :] += top_face * final


def call(kernel, shapes, *args):
    vmem = pl.BlockSpec(memory_space=pltpu.VMEM)
    return pl.pallas_call(
        kernel,
        out_shape=[jax.ShapeDtypeStruct(shape, F32) for shape in shapes],
        in_specs=[vmem] * len(args),
        out_specs=[vmem] * len(shapes),
        compiler_params=pltpu.CompilerParams(vmem_limit_bytes=32 * 1024 * 1024),
    )(*args)


def body(
    increment,
    blocks,
    face_weights,
    connected,
    overland_decay,
    river_cell,
    river_reach,
    river_count,
    inflow,
    outflow,
    storage,
):
    unknowns, layers, rows, cols = increment.shape
    x_rounds = log2(lax.axis_size("tx"))
    y_rounds = log2(lax.axis_size("ty"))
    decay = jnp.swapaxes(overland_decay, 1, 2)
    reach_rows = storage.shape[1] * lax.axis_size("tx") // LANES
    pad = -(-reach_rows // 8) * 8
    tall = -(-(unknowns + layers) // 8) * 8
    y_send, rims, x_send = call(
        send_kernel,
        [(2 + layers, tall, cols), (2, layers, tall, cols), (rows + 2 * pad, cols)],
        increment, decay, face_weights, connected, river_cell, river_reach, river_count, inflow, storage,
    )
    x_got = []
    y_got = []
    prior = jnp.stack([jnp.ones((tall, cols), F32), jnp.zeros((tall, cols), F32)])
    summed = lax.broadcasted_iota(jnp.int32, x_send.shape, 0) >= rows
    for k in range(max(x_rounds, y_rounds)):
        if k < y_rounds:
            y_got.append(swap(y_send, "ty", k))
        if k < x_rounds:
            x_got.append(swap(x_send, "tx", k))
            if k + 1 < x_rounds:
                x_send = x_send + jnp.where(summed, x_got[-1], 0.0)
        if k + 1 < y_rounds:
            y_send, prior = call(
                functools.partial(between_kernel, k, unknowns),
                [y_send.shape, prior.shape],
                y_send, y_got[-1], prior, rims,
            )
    part, grown = call(
        functools.partial(local_kernel, x_rounds, reach_rows),
        [increment.shape, decay.shape],
        increment, blocks, face_weights, connected, decay, river_cell, river_reach, river_count, outflow,
        x_send, *x_got,
    )
    (total,) = call(
        functools.partial(final_kernel, y_rounds),
        [increment.shape],
        part, grown, increment, face_weights, connected, prior, *y_got,
    )
    return total


def solution(mesh):
    in_specs = (
        P(None, None, "ty", "tx"),
        P(None, None, None, "ty", "tx"),
        P(None, None, "ty", "tx"),
        P(None, None, "ty", "tx"),
        P(None, "tx", "ty"),
        P("tx", "ty", None),
        P("tx", "ty", None),
        P("tx", "ty"),
        P("tx", "ty", None),
        P("tx", "ty", None),
        P("ty", "tx"),
    )
    out_specs = P(None, None, "ty", "tx")
    return jax.shard_map(body, mesh=mesh, in_specs=in_specs, out_specs=out_specs, check_vma=False)
```

```python
import functools
import jax
import jax.numpy as jnp
from jax import lax
from jax.experimental import pallas as pl
from jax.experimental.pallas import tpu as pltpu
from jax.sharding import PartitionSpec as P

F32 = jnp.float32
BF16 = jnp.bfloat16
LANES = 128


def log2(n):
    return n.bit_length() - 1


def bit_of(axis, k):
    return (lax.axis_index(axis) >> k) & 1


def split3(x):
    hi = x.astype(BF16).astype(F32)
    rest = x - hi
    mid = rest.astype(BF16).astype(F32)
    return hi, mid, rest - mid


def stack3(row, height):
    hi, mid, lo = split3(row)
    at = lax.broadcasted_iota(jnp.int32, (height, row.shape[1]), 0)
    zero = jnp.zeros((height, row.shape[1]), F32)
    out = jnp.where(at == 0, hi, jnp.where(at == 1, mid, jnp.where(at == 2, lo, zero)))
    return out.astype(BF16)


def hot(index_row, size, start=0):
    at = lax.broadcasted_iota(jnp.int32, (size, index_row.shape[1]), 0) + start
    return at == index_row


def fetch(pairs, sems):
    copies = [pltpu.make_async_copy(src, dst, sems.at[i]) for i, (src, dst) in enumerate(pairs)]
    for copy in copies:
        copy.start()
    return copies


def summary_kernel(inc_hbm, dec_hbm, fw_hbm, con_hbm, ysend_ref, inc_ref, dec_ref, fw_ref, con_ref, sems):
    unknowns, layers, rows, cols = inc_ref.shape
    tile = pl.ds(rows - fw_ref.shape[1], fw_ref.shape[1])
    copies = fetch(
        [
            (inc_hbm, inc_ref), (dec_hbm, dec_ref), (fw_hbm.at[1, :, tile, :], fw_ref),
            (con_hbm.at[1, :, tile, :], con_ref),
        ],
        sems,
    )
    ysend_ref[...] = jnp.zeros(ysend_ref.shape, F32)
    copies[0].wait()
    for layer in range(layers):
        ysend_ref[2 + layer, 0:unknowns] = inc_ref[:, layer, 0, :]
        ysend_ref[2 + layers + layer, 0:unknowns] = inc_ref[:, layer, rows - 1, :]
    copies[1].wait()
    product = dec_ref[:, 0, :]
    value = inc_ref[:, 0, 0, :]
    for y in range(1, rows):
        decay = dec_ref[:, y, :]
        product = product * decay
        value = value * decay + inc_ref[:, 0, y, :]
    ysend_ref[0, 0:unknowns] = product
    ysend_ref[1, 0:unknowns] = value
    copies[2].wait()
    copies[3].wait()
    for layer in range(layers):
        face = fw_ref[layer, -1:, :] * con_ref[layer, -1:, :].astype(F32)
        ysend_ref[2 + layers + layer, unknowns:unknowns + 1] = face


def river_rows(xsend_ref, rows, at, value):
    for c in range(value.shape[1] // LANES):
        xsend_ref[pl.ds(rows + at + c, 1), :] = value[:, c * LANES:(c + 1) * LANES]


def columns_kernel(
    pad, inc_hbm, fw_hbm, con_hbm, cell_hbm, reach_hbm, count_hbm, inflow_hbm, outflow_hbm, storage_hbm,
    xsend_ref, inc_ref, fw_ref, con_ref, cell_ref, reach_ref, count_ref, inflow_ref, outflow_ref, storage_ref, sems,
):
    copies = fetch(
        [
            (cell_hbm, cell_ref), (reach_hbm, reach_ref), (count_hbm, count_ref), (inflow_hbm, inflow_ref),
            (outflow_hbm, outflow_ref), (storage_hbm, storage_ref), (inc_hbm, inc_ref),
            (fw_hbm.at[0], fw_ref), (con_hbm.at[0], con_ref),
        ],
        sems,
    )
    unknowns, layers, rows, cols = inc_ref.shape
    xsend_ref[rows:, :] = jnp.zeros((xsend_ref.shape[0] - rows, LANES), F32)
    for copy in copies:
        copy.wait()
    cells = cell_ref[0]
    reaches = reach_ref[0]
    slots = cells.shape[1]
    wide = slots // LANES
    shift = log2(cols)
    parts = jnp.concatenate(split3(inc_ref[0, 0]), 0).astype(BF16)
    y_hot = hot(cells >> shift, rows).astype(F32)
    y_hot3 = jnp.concatenate([y_hot, y_hot, y_hot], 0).astype(BF16)
    picked = lax.dot_general(parts, y_hot3, (((0,), (0,)), ((), ())), preferred_element_type=F32)
    values = jnp.sum(jnp.where(hot(cells & (cols - 1), cols), picked, 0.0), 0, keepdims=True)
    live = lax.broadcasted_iota(jnp.int32, (1, slots), 1) < count_ref[...]
    terms = stack3(jnp.where(live, inflow_ref[0] * values, 0.0), 16)
    river_rows(xsend_ref, rows, 2 * pad, cells.astype(F32))
    river_rows(xsend_ref, rows, 2 * pad + wide, reaches.astype(F32))
    river_rows(xsend_ref, rows, 2 * pad + 2 * wide, jnp.where(live, outflow_ref[0], 0.0))
    reach_local = storage_ref.shape[1]
    x_index = lax.axis_index("tx")
    stored = jnp.concatenate([storage_ref[...]] * (LANES // reach_local), 1)
    owner = lax.broadcasted_iota(jnp.int32, (1, LANES), 1)
    for c in range(reach_local * lax.axis_size("tx") // LANES):
        r_hot = hot(reaches, LANES, c * LANES).astype(F32).astype(BF16)
        total = lax.dot_general(terms, r_hot, (((1,), (1,)), ((), ())), preferred_element_type=F32)
        xsend_ref[pl.ds(rows + c, 1), :] = jnp.sum(total, 0, keepdims=True)
        xsend_ref[pl.ds(rows + pad + c, 1), :] = jnp.where(
            (owner + c * LANES) // reach_local == x_index, stored, 0.0
        )
    pair = lax.broadcasted_iota(jnp.int32, (rows, cols), 1) >> 1
    packed = jnp.zeros((rows, cols), F32)
    for p in range(unknowns * layers + layers):
        if p < unknowns * layers:
            plane = inc_ref[p // layers, p % layers]
        else:
            layer = p - unknowns * layers
            plane = fw_ref[layer] * con_ref[layer].astype(F32)
        packed = jnp.where(pair == p, pltpu.roll(plane, 2 * p + 1, 1), packed)
    xsend_ref[0:rows, :] = packed


def prefix_step(k, received, prior):
    upper = bit_of("ty", k) == 1
    if prior is None:
        return jnp.where(upper, received[0], 1.0), jnp.where(upper, received[1], 0.0)
    product = jnp.where(upper, prior[0] * received[0], prior[0])
    value = jnp.where(upper, prior[0] * received[1] + prior[1], prior[1])
    return product, value


def between_kernel(k, layers, sums, sent_ref, got_ref, *refs):
    refs = list(refs)
    prior_ref = refs.pop(0) if k > 0 else None
    if sums is not None:
        xsent_ref, xgot_ref = refs[:2]
        xsend_ref = refs.pop()
        start, stop = sums
        xsend_ref[...] = xsent_ref[...]
        xsend_ref[start:stop, :] = xsent_ref[start:stop, :] + xgot_ref[start:stop, :]
    send_ref, next_ref = refs[-2:]
    upper = bit_of("ty", k) == 1
    product, value = prefix_step(k, got_ref, prior_ref)
    next_ref[0] = product
    next_ref[1] = value
    own_a, own_b, got_a, got_b = sent_ref[0], sent_ref[1], got_ref[0], got_ref[1]
    low_b = jnp.where(upper, got_b, own_b)
    up_a = jnp.where(upper, own_a, got_a)
    up_b = jnp.where(upper, own_b, got_b)
    send_ref[0] = own_a * got_a
    send_ref[1] = up_a * low_b + up_b
    for layer in range(layers):
        passed = got_ref[2 + layer]
        if k == 0:
            passed = jnp.where(upper, passed, got_ref[2 + layers + layer])
        send_ref[2 + layer] = passed


def beside_x(received, rows):
    index = lax.axis_index("tx")
    below = jnp.zeros((rows, LANES), F32)
    above = below
    for k, buffer in enumerate(received):
        low = (1 << k) - 1
        full = (2 << k) - 1
        above = jnp.where((index & full) == low, buffer[0:rows, :], above)
        below = jnp.where((index & full) == low + 1, buffer[0:rows, :], below)
    return below, above


def local_kernel(x_rounds, pad, reach_rows, slots, *refs):
    blocks_hbm, inc_hbm, dec_hbm, fw_hbm, con_hbm, sent_ref = refs[:6]
    received = refs[6:6 + x_rounds]
    inc_ref, dec_ref, fw_ref, con_ref, blocks_ref, value_ref, product_ref, sems = refs[-8:]
    unknowns, layers, rows, cols = inc_ref.shape
    out_refs = refs[6 + x_rounds:6 + x_rounds + unknowns]
    grown_refs = refs[6 + x_rounds + unknowns:6 + x_rounds + 2 * unknowns]
    copies = fetch(
        [(inc_hbm, inc_ref), (dec_hbm, dec_ref), (fw_hbm, fw_ref), (con_hbm, con_ref)]
        + [(blocks_hbm.at[i], blocks_ref.at[i]) for i in range(unknowns)],
        sems,
    )
    lane = lax.broadcasted_iota(jnp.int32, (rows, cols), 1)
    row = lax.broadcasted_iota(jnp.int32, (rows, cols), 0)
    wide = slots // LANES

    def slot_row(at):
        start = rows + 2 * pad + at * wide
        return jnp.concatenate([sent_ref[start + c:start + c + 1, :] for c in range(wide)], 1)

    cells = slot_row(0).astype(jnp.int32)
    reaches = slot_row(1).astype(jnp.int32)
    totals = sent_ref[rows:rows + pad, :] + received[-1][rows:rows + pad, :]
    storage = sent_ref[rows + pad:rows + 2 * pad, :] + received[-1][rows + pad:rows + 2 * pad, :]
    shift = log2(cols)
    picked = jnp.zeros((16, slots), F32)
    for c in range(reach_rows):
        section = stack3(totals[c:c + 1] / storage[c:c + 1], 16)
        r_hot = hot(reaches, LANES, c * LANES).astype(F32).astype(BF16)
        picked = picked + lax.dot_general(section, r_hot, (((1,), (0,)), ((), ())), preferred_element_type=F32)
    back = slot_row(2) * jnp.sum(picked, 0, keepdims=True)
    y_hot = hot(cells >> shift, rows)
    spread = jnp.concatenate([jnp.where(y_hot, part, 0.0) for part in split3(back)], 0).astype(BF16)
    x_hot = hot(cells & (cols - 1), cols).astype(F32).astype(BF16)
    added = lax.dot_general(spread, x_hot, (((1,), (1,)), ((), ())), preferred_element_type=F32)
    river = added[0:rows] + added[rows:2 * rows] + added[2 * rows:3 * rows]
    copies[0].wait()
    copies[1].wait()
    product = 0.1 * dec_ref[:, 0, :]
    value = 0.1 * inc_ref[:, 0, 0, :]
    product_ref[:, 0, :] = product
    value_ref[:, 0, :] = value
    for y in range(1, rows):
        decay = dec_ref[:, y, :]
        product = product * decay
        value = value * decay + 0.1 * inc_ref[:, 0, y, :]
        product_ref[:, y, :] = product
        value_ref[:, y, :] = value
    copies[2].wait()
    copies[3].wait()
    left, right = beside_x(received, rows)
    rim = jnp.where(lane & 1 == 0, pltpu.roll(right, cols - 1, 1), pltpu.roll(left, 1, 1))
    planes = unknowns * layers
    for u in range(unknowns):
        grown_refs[u][...] = product_ref[u]
        copies[4 + u].wait()
        for layer in range(layers):
            face_x = fw_ref[0, layer] * con_ref[0, layer].astype(F32)
            face_y = jnp.where(row == rows - 1, 0.0, fw_ref[1, layer] * con_ref[1, layer].astype(F32))
            face_z = fw_ref[2, layer] * con_ref[2, layer].astype(F32)
            face_left = pltpu.roll(rim, (cols - 1 - 2 * (planes + layer)) % cols, 1)
            here = inc_ref[u, layer]
            p = u * layers + layer
            beside = pltpu.roll(rim, cols - 1 - 2 * p, 1)
            flow_x = face_x * (here - jnp.where(lane == cols - 1, beside, pltpu.roll(here, cols - 1, 1)))
            from_left = jnp.where(lane == 0, face_left * (beside - here), pltpu.roll(flow_x, 1, 1))
            flow_y = face_y * (here - pltpu.roll(here, rows - 1, 0))
            total = flow_x - from_left + (flow_y - pltpu.roll(flow_y, 1, 0))
            if layer + 1 < layers:
                total = total + face_z * (here - inc_ref[u, layer + 1])
            else:
                total = total + face_z * here
            if layer > 0:
                face_above = fw_ref[2, layer - 1] * con_ref[2, layer - 1].astype(F32)
                total = total + face_above * (here - inc_ref[u, layer - 1])
            else:
                total = total + value_ref[u]
                if u == 0:
                    total = total + river
            for j in range(unknowns):
                total = total + blocks_ref[u, j, layer].astype(F32) * inc_ref[j, layer]
            out_refs[u][layer] = total


def final_kernel(unknowns, y_rounds, *refs):
    part_refs = refs[:unknowns]
    grown_refs = refs[unknowns:2 * unknowns]
    own_ref = refs[2 * unknowns]
    got = refs[2 * unknowns + 1:2 * unknowns + 1 + y_rounds]
    prior_ref, out_ref = refs[-2:]
    layers, rows, cols = part_refs[0].shape
    _, carry = prefix_step(y_rounds - 1, got[-1], prior_ref)
    index = lax.axis_index("ty")
    odd = (index & 1) == 1
    at = lax.broadcasted_iota(jnp.int32, (8, cols), 0)
    starts = []
    ends = []
    for layer in range(layers):
        passed_up = jnp.zeros(carry.shape, F32)
        passed_down = passed_up
        for k in range(1, y_rounds):
            full = (2 << k) - 1
            passed_up = jnp.where((index & full) == (1 << k), got[k][2 + layer], passed_up)
            passed_down = jnp.where((index & full) == (1 << k) - 1, got[k][2 + layer], passed_down)
        below = jnp.where(odd, got[0][2 + layers + layer], passed_up)
        above = jnp.where(odd, passed_down, got[0][2 + layer])
        low_face = below[unknowns:unknowns + 1]
        top_face = own_ref[2 + layers + layer, unknowns:unknowns + 1]
        starts.append(low_face * (own_ref[2 + layer] - below))
        ends.append(top_face * (own_ref[2 + layers + layer] - above))
    for u in range(unknowns):
        for layer in range(layers):
            total = part_refs[u][layer]
            if layer == 0:
                total = total + grown_refs[u][...] * carry[u:u + 1]
            head = total[0:8] + jnp.where(at == 0, starts[layer][u:u + 1], 0.0)
            foot = total[rows - 8:rows] + jnp.where(at == 7, ends[layer][u:u + 1], 0.0)
            out_ref[u, layer, 0:8, :] = head
            out_ref[u, layer, 8:rows - 8, :] = total[8:rows - 8]
            out_ref[u, layer, rows - 8:rows, :] = foot


def call(kernel, outs, args, far=0, scratch=(), grant=32 * 1024, cost=0):
    vmem = pl.BlockSpec(memory_space=pltpu.VMEM)
    hbm = pl.BlockSpec(memory_space=pltpu.HBM)
    return pl.pallas_call(
        kernel,
        out_shape=[jax.ShapeDtypeStruct(o.shape, o.dtype) for o in outs],
        in_specs=[hbm] * far + [vmem] * (len(args) - far),
        out_specs=[vmem] * len(outs),
        scratch_shapes=list(scratch),
        compiler_params=pltpu.CompilerParams(vmem_limit_bytes=grant * 1024),
        cost_estimate=pl.CostEstimate(flops=0, bytes_accessed=cost, transcendentals=0),
    )(*args)


def f32(*shape):
    return jax.ShapeDtypeStruct(shape, F32)


def like(a, *shape):
    return pltpu.VMEM(shape or a.shape, a.dtype)


SUMMARY_GRANT = 55160
COLUMNS_GRANT = 56000
LOCAL_GRANT = 54440
LOCAL_COST = 0
COLUMNS_COST = 0


def body(
    increment,
    blocks,
    face_weights,
    connected,
    overland_decay,
    river_cell,
    river_reach,
    river_count,
    inflow,
    outflow,
    storage,
):
    unknowns, layers, rows, cols = increment.shape
    x_size = lax.axis_size("tx")
    y_size = lax.axis_size("ty")
    x_rounds = log2(x_size)
    y_rounds = log2(y_size)
    slots = river_cell.shape[2]
    decay = jnp.swapaxes(overland_decay, 1, 2)
    reach_rows = storage.shape[1] * x_size // LANES
    pad = -(-reach_rows // 8) * 8
    tall = -(-(unknowns + 1) // 8) * 8
    edge = (layers, 8, cols)
    (y_first,) = call(
        summary_kernel,
        [f32(2 + 2 * layers, tall, cols)],
        [increment, decay, face_weights, connected],
        far=4,
        scratch=[
            like(increment), like(decay), like(face_weights, *edge), like(connected, *edge),
            pltpu.SemaphoreType.DMA((4,)),
        ],
        grant=SUMMARY_GRANT,
    )
    args = [
        increment, face_weights, connected, river_cell, river_reach, river_count, inflow, outflow, storage,
    ]
    (x_send,) = call(
        functools.partial(columns_kernel, pad),
        [f32(rows + 2 * pad + -(-3 * slots // LANES // 8) * 8, cols)],
        args,
        far=len(args),
        scratch=[like(increment)]
        + [like(a, layers, rows, cols) for a in args[1:3]]
        + [like(a) for a in args[3:]]
        + [pltpu.SemaphoreType.DMA((len(args),))],
        grant=COLUMNS_GRANT,
        cost=COLUMNS_COST,
    )
    y_send = y_first
    y_got = []
    x_got = []
    prior = None
    for k in range(max(x_rounds, y_rounds)):
        more_x = k + 1 < x_rounds
        more_y = k + 1 < y_rounds
        if k < y_rounds:
            y_got.append(lax.ppermute(y_send, "ty", [(i, i ^ (1 << k)) for i in range(y_size)]))
        if k < x_rounds:
            x_got.append(lax.ppermute(x_send, "tx", [(i, i ^ ((2 << k) - 1)) for i in range(x_size)]))
        if more_x or more_y:
            made = call(
                functools.partial(between_kernel, k, layers, (rows, rows + 2 * pad) if more_x else None),
                [f32(2 + layers, tall, cols), f32(2, tall, cols)] + ([x_send] if more_x else []),
                [y_send, y_got[-1]]
                + ([prior] if k > 0 else [])
                + ([x_send] if more_x else [])
                + (x_got[-1:] if k < x_rounds else []),
            )
            y_send, prior = made[:2]
            if more_x:
                x_send = made[2]
    local = call(
        functools.partial(local_kernel, x_rounds, pad, reach_rows, slots),
        [f32(layers, rows, cols)] * unknowns + [f32(rows, cols)] * unknowns,
        [blocks, increment, decay, face_weights, connected, x_send, *x_got],
        far=5,
        scratch=[
            like(increment), like(decay), like(face_weights), like(connected), like(blocks), like(decay), like(decay),
            pltpu.SemaphoreType.DMA((4 + unknowns,)),
        ],
        grant=LOCAL_GRANT,
        cost=LOCAL_COST,
    )
    (total,) = call(
        functools.partial(final_kernel, unknowns, y_rounds),
        [increment],
        [*local, y_first, *y_got, prior],
    )
    return total


def solution(mesh):
    in_specs = (
        P(None, None, "ty", "tx"),
        P(None, None, None, "ty", "tx"),
        P(None, None, "ty", "tx"),
        P(None, None, "ty", "tx"),
        P(None, "tx", "ty"),
        P("tx", "ty", None),
        P("tx", "ty", None),
        P("tx", "ty"),
        P("tx", "ty", None),
        P("tx", "ty", None),
        P("ty", "tx"),
    )
    out_specs = P(None, None, "ty", "tx")
    return jax.shard_map(body, mesh=mesh, in_specs=in_specs, out_specs=out_specs, check_vma=False)
```

```python
import functools
import jax
import jax.numpy as jnp
from jax import lax
from jax.experimental import pallas as pl
from jax.experimental.pallas import tpu as pltpu
from jax.sharding import PartitionSpec as P

F32 = jnp.float32
BF16 = jnp.bfloat16
LANES = 128


def log2(n):
    return n.bit_length() - 1


def bit_of(axis, k):
    return (lax.axis_index(axis) >> k) & 1


def split3(x):
    hi = x.astype(BF16).astype(F32)
    rest = x - hi
    mid = rest.astype(BF16).astype(F32)
    return hi, mid, rest - mid


def stack3(row, height):
    hi, mid, lo = split3(row)
    at = lax.broadcasted_iota(jnp.int32, (height, row.shape[1]), 0)
    zero = jnp.zeros((height, row.shape[1]), F32)
    out = jnp.where(at == 0, hi, jnp.where(at == 1, mid, jnp.where(at == 2, lo, zero)))
    return out.astype(BF16)


def hot(index_row, size, start=0):
    at = lax.broadcasted_iota(jnp.int32, (size, index_row.shape[1]), 0) + start
    return at == index_row


def fetch(pairs, sems):
    copies = [pltpu.make_async_copy(src, dst, sems.at[i]) for i, (src, dst) in enumerate(pairs)]
    for copy in copies:
        copy.start()
    return copies


def summary_kernel(unknowns, inc_hbm, dec_hbm, fw_hbm, con_hbm, ysend_ref, packed_ref, *refs):
    inc_out = refs[:unknowns]
    face_out = refs[unknowns:-5]
    inc_ref, dec_ref, fw_ref, con_ref, sems = refs[-5:]
    _, layers, rows, cols = inc_ref.shape
    copies = fetch([(inc_hbm, inc_ref), (dec_hbm, dec_ref), (fw_hbm, fw_ref), (con_hbm, con_ref)], sems)
    ysend_ref[...] = jnp.zeros(ysend_ref.shape, F32)
    for copy in copies:
        copy.wait()
    product = dec_ref[:, 0, :]
    value = inc_ref[:, 0, 0, :]
    for y in range(1, rows):
        decay = dec_ref[:, y, :]
        product = product * decay
        value = value * decay + inc_ref[:, 0, y, :]
    pair = lax.broadcasted_iota(jnp.int32, (rows, cols), 1) >> 1
    row = lax.broadcasted_iota(jnp.int32, (rows, cols), 0)
    packed = jnp.zeros((rows, cols), F32)
    planes = unknowns * layers
    for p in range(planes):
        packed = jnp.where(pair == p, pltpu.roll(inc_ref[p // layers, p % layers], 2 * p + 1, 1), packed)
    faces = [[fw_ref[d, l] * con_ref[d, l].astype(F32) for l in range(layers)] for d in range(3)]
    for layer in range(layers):
        p = planes + layer
        packed = jnp.where(pair == p, pltpu.roll(faces[0][layer], 2 * p + 1, 1), packed)
    ysend_ref[0, 0:unknowns] = product
    ysend_ref[1, 0:unknowns] = value
    for layer in range(layers):
        ysend_ref[2 + layer, 0:unknowns] = inc_ref[:, layer, 0, :]
        ysend_ref[2 + layers + layer, 0:unknowns] = inc_ref[:, layer, rows - 1, :]
        ysend_ref[2 + layers + layer, unknowns:unknowns + 1] = faces[1][layer][rows - 1:]
        face_out[layer][...] = faces[0][layer]
        face_out[layers + layer][...] = jnp.where(row == rows - 1, 0.0, faces[1][layer])
        face_out[2 * layers + layer][...] = faces[2][layer]
    packed_ref[...] = packed
    for u in range(unknowns):
        inc_out[u][...] = inc_ref[u]


def river_rows(xsend_ref, rows, at, value):
    for c in range(value.shape[1] // LANES):
        xsend_ref[pl.ds(rows + at + c, 1), :] = value[:, c * LANES:(c + 1) * LANES]


def river_kernel(pad, reach_local, code_ref, outflow_ref, inflow_ref, storage_ref, packed_ref, inc_ref, _, xsend_ref):
    layers, rows, cols = inc_ref.shape
    slots = code_ref.shape[2]
    wide = slots // LANES
    code = code_ref[0].astype(jnp.int32)
    reaches = code >> log2(rows * cols)
    cells = code & (rows * cols - 1)
    xsend_ref[rows:, :] = jnp.zeros((xsend_ref.shape[0] - rows, LANES), F32)
    xsend_ref[0:rows, :] = packed_ref[...]
    river_rows(xsend_ref, rows, 2 * pad, cells.astype(F32))
    river_rows(xsend_ref, rows, 2 * pad + wide, reaches.astype(F32))
    river_rows(xsend_ref, rows, 2 * pad + 2 * wide, outflow_ref[0])
    y_hot = hot(cells >> log2(cols), rows).astype(F32)
    y_hot3 = jnp.concatenate([y_hot, y_hot, y_hot], 0).astype(BF16)
    parts = jnp.concatenate(split3(inc_ref[0]), 0).astype(BF16)
    picked = lax.dot_general(parts, y_hot3, (((0,), (0,)), ((), ())), preferred_element_type=F32)
    values = jnp.sum(jnp.where(hot(cells & (cols - 1), cols), picked, 0.0), 0, keepdims=True)
    terms = stack3(inflow_ref[0] * values, 16)
    x_index = lax.axis_index("tx")
    owner = lax.broadcasted_iota(jnp.int32, (1, LANES), 1)
    stored = jnp.concatenate([storage_ref[0, :, 0:reach_local]] * (LANES // reach_local), 1)
    for c in range(reach_local * lax.axis_size("tx") // LANES):
        r_hot = hot(reaches, LANES, c * LANES).astype(F32).astype(BF16)
        total = lax.dot_general(terms, r_hot, (((1,), (1,)), ((), ())), preferred_element_type=F32)
        xsend_ref[pl.ds(rows + c, 1), :] = jnp.sum(total, 0, keepdims=True)
        xsend_ref[pl.ds(rows + pad + c, 1), :] = jnp.where(
            (owner + c * LANES) // reach_local == x_index, stored, 0.0
        )


def prefix_step(k, received, prior):
    upper = bit_of("ty", k) == 1
    if prior is None:
        return jnp.where(upper, received[0], 1.0), jnp.where(upper, received[1], 0.0)
    product = jnp.where(upper, prior[0] * received[0], prior[0])
    value = jnp.where(upper, prior[0] * received[1] + prior[1], prior[1])
    return product, value


def between_kernel(k, layers, sent_ref, got_ref, *refs):
    prior_ref = refs[0] if k > 0 else None
    send_ref, next_ref = refs[-2:]
    upper = bit_of("ty", k) == 1
    product, value = prefix_step(k, got_ref, prior_ref)
    next_ref[0] = product
    next_ref[1] = value
    own_a, own_b, got_a, got_b = sent_ref[0], sent_ref[1], got_ref[0], got_ref[1]
    low_b = jnp.where(upper, got_b, own_b)
    up_a = jnp.where(upper, own_a, got_a)
    up_b = jnp.where(upper, own_b, got_b)
    send_ref[0] = own_a * got_a
    send_ref[1] = up_a * low_b + up_b
    for layer in range(layers):
        passed = got_ref[2 + layer]
        if k == 0:
            passed = jnp.where(upper, passed, got_ref[2 + layers + layer])
        send_ref[2 + layer] = passed


def beside_x(received, rows):
    index = lax.axis_index("tx")
    below = jnp.zeros((rows, LANES), F32)
    above = below
    for k, buffer in enumerate(received):
        low = (1 << k) - 1
        full = (2 << k) - 1
        above = jnp.where((index & full) == low, buffer[0:rows, :], above)
        below = jnp.where((index & full) == low + 1, buffer[0:rows, :], below)
    return below, above


def multiply(u, blocks, inc_refs, total):
    for j in range(len(inc_refs)):
        total = total + blocks[j].astype(F32) * inc_refs[j][...]
    return total


def ahead_kernel(unknowns, count, blocks_hbm, *refs):
    inc_refs = refs[1:1 + unknowns]
    out_refs = refs[1 + unknowns:-2]
    blocks_ref, sems = refs[-2:]
    copies = fetch([(blocks_hbm.at[i], blocks_ref.at[i]) for i in range(count)], sems)
    for u in range(count):
        if u % WAITS == 0:
            for copy in copies[u:u + WAITS]:
                copy.wait()
        out_refs[u][...] = multiply(u, blocks_ref.at[u], inc_refs, jnp.zeros(out_refs[u].shape, F32))


def local_kernel(x_rounds, pad, reach_rows, slots, unknowns, layers, count, blocks_hbm, inc_hbm, dec_hbm, sent_ref, *refs):
    received, refs = refs[:x_rounds], refs[x_rounds:]
    inc_refs, refs = refs[:unknowns], refs[unknowns:]
    face_refs, refs = refs[:3 * layers], refs[3 * layers:]
    done_refs, refs = refs[:count], refs[count:]
    out_refs, refs = refs[:unknowns], refs[unknowns:]
    grown_refs, refs = refs[:unknowns], refs[unknowns:]
    blocks_ref, flux_ref, top_ref, dec_ref, value_ref, product_ref, sems = refs
    _, rows, cols = inc_refs[0].shape
    copies = fetch(
        [(inc_hbm.at[:, 0], top_ref), (dec_hbm, dec_ref)]
        + [(blocks_hbm.at[i], blocks_ref.at[i - count]) for i in range(count, unknowns)],
        sems,
    )
    lane = lax.broadcasted_iota(jnp.int32, (rows, cols), 1)
    wide = slots // LANES

    def slot_row(at):
        start = rows + 2 * pad + at * wide
        return jnp.concatenate([sent_ref[start + c:start + c + 1, :] for c in range(wide)], 1)

    cells = slot_row(0).astype(jnp.int32)
    reaches = slot_row(1).astype(jnp.int32)
    totals = sent_ref[rows:rows + pad, :] + received[-1][rows:rows + pad, :]
    storage = sent_ref[rows + pad:rows + 2 * pad, :] + received[-1][rows + pad:rows + 2 * pad, :]
    shift = log2(cols)
    picked = jnp.zeros((16, slots), F32)
    for c in range(reach_rows):
        section = stack3(totals[c:c + 1] / storage[c:c + 1], 16)
        r_hot = hot(reaches, LANES, c * LANES).astype(F32).astype(BF16)
        picked = picked + lax.dot_general(section, r_hot, (((1,), (0,)), ((), ())), preferred_element_type=F32)
    back = slot_row(2) * jnp.sum(picked, 0, keepdims=True)
    y_hot = hot(cells >> shift, rows)
    spread = jnp.concatenate([jnp.where(y_hot, part, 0.0) for part in split3(back)], 0).astype(BF16)
    x_hot = hot(cells & (cols - 1), cols).astype(F32).astype(BF16)
    added = lax.dot_general(spread, x_hot, (((1,), (1,)), ((), ())), preferred_element_type=F32)
    river = added[0:rows] + added[rows:2 * rows] + added[2 * rows:3 * rows]
    left, right = beside_x(received, rows)
    rim = jnp.where(lane & 1 == 0, pltpu.roll(right, cols - 1, 1), pltpu.roll(left, 1, 1))
    planes = unknowns * layers
    for layer in range(layers):
        face_x = face_refs[layer][...]
        face_y = face_refs[layers + layer][...]
        face_z = face_refs[2 * layers + layer][...]
        face_left = pltpu.roll(rim, (cols - 1 - 2 * (planes + layer)) % cols, 1)
        for first in range(0, unknowns, GROUP):
            group = range(first, min(first + GROUP, unknowns))
            here = jnp.stack([inc_refs[u][layer] for u in group])
            beside = jnp.stack([pltpu.roll(rim, cols - 1 - 2 * (u * layers + layer), 1) for u in group])
            flow_x = face_x * (here - jnp.where(lane == cols - 1, beside, pltpu.roll(here, cols - 1, 2)))
            from_left = jnp.where(lane == 0, face_left * (beside - here), pltpu.roll(flow_x, 1, 2))
            flow_y = face_y * (here - pltpu.roll(here, rows - 1, 1))
            total = flow_x - from_left + (flow_y - pltpu.roll(flow_y, 1, 1))
            if layer + 1 < layers:
                total = total + face_z * (here - jnp.stack([inc_refs[u][layer + 1] for u in group]))
            else:
                total = total + face_z * here
            if layer > 0:
                over = jnp.stack([inc_refs[u][layer - 1] for u in group])
                total = total + face_refs[2 * layers + layer - 1][...] * (here - over)
            for u in group:
                flux_ref[u, layer] = total[u - first] + river if u + layer == 0 else total[u - first]
    copies[0].wait()
    copies[1].wait()
    product = 0.1 * dec_ref[:, 0, :]
    value = 0.1 * top_ref[:, 0, :]
    product_ref[:, 0, :] = product
    value_ref[:, 0, :] = value
    for y in range(1, rows):
        decay = dec_ref[:, y, :]
        product = product * decay
        value = value * decay + 0.1 * top_ref[:, y, :]
        product_ref[:, y, :] = product
        value_ref[:, y, :] = value
    for u in range(unknowns):
        total = flux_ref[u]
        if u < count:
            total = total + done_refs[u][...]
        else:
            at = u - count
            if at % WAITS == 0:
                for copy in copies[2 + at:2 + at + WAITS]:
                    copy.wait()
            total = multiply(u, blocks_ref.at[at], inc_refs, total)
        out_refs[u][0] = total[0] + value_ref[u]
        out_refs[u][1:] = total[1:]
        grown_refs[u][...] = product_ref[u]


def final_kernel(unknowns, y_rounds, *refs):
    part_refs = refs[:unknowns]
    grown_refs = refs[unknowns:2 * unknowns]
    own_ref = refs[2 * unknowns]
    got = refs[2 * unknowns + 1:2 * unknowns + 1 + y_rounds]
    prior_ref, out_ref = refs[-2:]
    layers, rows, cols = part_refs[0].shape
    _, carry = prefix_step(y_rounds - 1, got[-1], prior_ref)
    index = lax.axis_index("ty")
    odd = (index & 1) == 1
    at = lax.broadcasted_iota(jnp.int32, (8, cols), 0)
    starts = []
    ends = []
    for layer in range(layers):
        passed_up = jnp.zeros(carry.shape, F32)
        passed_down = passed_up
        for k in range(1, y_rounds):
            full = (2 << k) - 1
            passed_up = jnp.where((index & full) == (1 << k), got[k][2 + layer], passed_up)
            passed_down = jnp.where((index & full) == (1 << k) - 1, got[k][2 + layer], passed_down)
        below = jnp.where(odd, got[0][2 + layers + layer], passed_up)
        above = jnp.where(odd, passed_down, got[0][2 + layer])
        low_face = below[unknowns:unknowns + 1]
        top_face = own_ref[2 + layers + layer, unknowns:unknowns + 1]
        starts.append(low_face * (own_ref[2 + layer] - below))
        ends.append(top_face * (own_ref[2 + layers + layer] - above))
    for u in range(unknowns):
        for layer in range(layers):
            total = part_refs[u][layer]
            if layer == 0:
                total = total + grown_refs[u][...] * carry[u:u + 1]
            head = total[0:8] + jnp.where(at == 0, starts[layer][u:u + 1], 0.0)
            foot = total[rows - 8:rows] + jnp.where(at == 7, ends[layer][u:u + 1], 0.0)
            out_ref[u, layer, 0:8, :] = head
            out_ref[u, layer, 8:rows - 8, :] = total[8:rows - 8]
            out_ref[u, layer, rows - 8:rows, :] = foot


def call(kernel, outs, args, far=0, scratch=(), grant=32 * 1024, cost=0):
    vmem = pl.BlockSpec(memory_space=pltpu.VMEM)
    hbm = pl.BlockSpec(memory_space=pltpu.HBM)
    return pl.pallas_call(
        kernel,
        out_shape=[jax.ShapeDtypeStruct(o.shape, o.dtype) for o in outs],
        in_specs=[hbm] * far + [vmem] * (len(args) - far),
        out_specs=[vmem] * len(outs),
        scratch_shapes=list(scratch),
        compiler_params=pltpu.CompilerParams(vmem_limit_bytes=grant * 1024),
        cost_estimate=pl.CostEstimate(flops=0, bytes_accessed=cost, transcendentals=0),
    )(*args)


def f32(*shape):
    return jax.ShapeDtypeStruct(shape, F32)


def like(a, *shape):
    return pltpu.VMEM(shape or a.shape, a.dtype)


SUMMARY_GRANT = 54600
LOCAL_GRANT = 53725
LOCAL_COST = 0
RIVER_COST = 0
GROUP = 7
WAITS = 3
AHEAD = 6
AHEAD_GRANT = 52000


def body(
    increment,
    blocks,
    face_weights,
    connected,
    overland_decay,
    river_cell,
    river_reach,
    river_count,
    inflow,
    outflow,
    storage,
):
    unknowns, layers, rows, cols = increment.shape
    x_size = lax.axis_size("tx")
    y_size = lax.axis_size("ty")
    x_rounds = log2(x_size)
    y_rounds = log2(y_size)
    slots = river_cell.shape[2]
    decay = jnp.swapaxes(overland_decay, 1, 2)
    reach_rows = storage.shape[1] * x_size // LANES
    pad = -(-reach_rows // 8) * 8
    tall = -(-(unknowns + 1) // 8) * 8
    plane = f32(rows, cols)
    y_first, packed, *kept = call(
        functools.partial(summary_kernel, unknowns),
        [f32(2 + 2 * layers, tall, cols), plane] + [f32(layers, rows, cols)] * unknowns + [plane] * (3 * layers),
        [increment, decay, face_weights, connected],
        far=4,
        scratch=[
            like(increment), like(decay), like(face_weights), like(connected), pltpu.SemaphoreType.DMA((4,)),
        ],
        grant=SUMMARY_GRANT,
    )
    live = lax.broadcasted_iota(jnp.int32, river_cell.shape, 2) < river_count[:, :, None]
    code = jnp.where(live, (river_cell + (rows * cols) * river_reach).astype(F32), 0.0)
    reach_local = storage.shape[1]
    stored = jnp.pad(storage[None], ((0, 0), (0, 0), (0, slots - reach_local)))
    stored = jnp.where(lax.broadcasted_iota(jnp.int32, stored.shape, 2) < reach_local, stored, jnp.where(live, 1.0, 0.0))
    (x_send,) = call(
        functools.partial(river_kernel, pad, reach_local),
        [f32(rows + 2 * pad + -(-3 * slots // LANES // 8) * 8, cols)],
        [code, jnp.where(live, outflow, 0.0), jnp.where(live, inflow, 0.0), stored, packed, kept[0], y_first],
        cost=RIVER_COST,
    )
    y_send = y_first
    y_got = []
    x_got = []
    prior = None
    at = lax.broadcasted_iota(jnp.int32, x_send.shape, 0)
    summed = (at >= rows) & (at < rows + 2 * pad)
    for k in range(max(x_rounds, y_rounds)):
        if k < y_rounds:
            y_got.append(lax.ppermute(y_send, "ty", [(i, i ^ (1 << k)) for i in range(y_size)]))
        if k < x_rounds:
            x_got.append(lax.ppermute(x_send, "tx", [(i, i ^ ((2 << k) - 1)) for i in range(x_size)]))
            if k + 1 < x_rounds:
                x_send = x_send + jnp.where(summed, x_got[-1], 0.0)
        if k + 1 < y_rounds:
            y_send, prior = call(
                functools.partial(between_kernel, k, layers),
                [f32(2 + layers, tall, cols), f32(2, tall, cols)],
                [y_send, y_got[-1]] + ([prior] + x_got[k:k + 1] + list(ahead[:1]) if k > 0 else []),
            )
            if k == 0:
                ahead = call(
                    functools.partial(ahead_kernel, unknowns, AHEAD),
                    [f32(layers, rows, cols)] * AHEAD,
                    [blocks, y_send, *kept[:unknowns]],
                    far=1,
                    scratch=[like(blocks, AHEAD, *blocks.shape[1:]), pltpu.SemaphoreType.DMA((AHEAD,))],
                    grant=AHEAD_GRANT,
                )
    local = call(
        functools.partial(local_kernel, x_rounds, pad, reach_rows, slots, unknowns, layers, AHEAD),
        [f32(layers, rows, cols)] * unknowns + [plane] * unknowns,
        [blocks, increment, decay, x_send, *x_got, *kept, *ahead],
        far=3,
        scratch=[
            like(blocks, unknowns - AHEAD, *blocks.shape[1:]), like(increment), like(decay), like(decay), like(decay), like(decay), pltpu.SemaphoreType.DMA((2 + unknowns - AHEAD,)),
        ],
        grant=LOCAL_GRANT,
        cost=LOCAL_COST,
    )
    (total,) = call(
        functools.partial(final_kernel, unknowns, y_rounds),
        [increment],
        [*local, y_first, *y_got, prior],
    )
    return total


def solution(mesh):
    in_specs = (
        P(None, None, "ty", "tx"),
        P(None, None, None, "ty", "tx"),
        P(None, None, "ty", "tx"),
        P(None, None, "ty", "tx"),
        P(None, "tx", "ty"),
        P("tx", "ty", None),
        P("tx", "ty", None),
        P("tx", "ty"),
        P("tx", "ty", None),
        P("tx", "ty", None),
        P("ty", "tx"),
    )
    out_specs = P(None, None, "ty", "tx")
    return jax.shard_map(body, mesh=mesh, in_specs=in_specs, out_specs=out_specs, check_vma=False)
```

```python
import functools
import jax
import jax.numpy as jnp
from jax import lax
from jax.experimental import pallas as pl
from jax.experimental.pallas import tpu as pltpu
from jax.sharding import PartitionSpec as P

F32 = jnp.float32
BF16 = jnp.bfloat16
LANES = 128


def log2(n):
    return n.bit_length() - 1


def bit_of(axis, k):
    return (lax.axis_index(axis) >> k) & 1


def split3(x):
    hi = x.astype(BF16).astype(F32)
    rest = x - hi
    mid = rest.astype(BF16).astype(F32)
    return hi, mid, rest - mid


def stack3(row, height):
    hi, mid, lo = split3(row)
    at = lax.broadcasted_iota(jnp.int32, (height, row.shape[1]), 0)
    zero = jnp.zeros((height, row.shape[1]), F32)
    out = jnp.where(at == 0, hi, jnp.where(at == 1, mid, jnp.where(at == 2, lo, zero)))
    return out.astype(BF16)


def hot(index_row, size, start=0):
    at = lax.broadcasted_iota(jnp.int32, (size, index_row.shape[1]), 0) + start
    return at == index_row


def fetch(pairs, sems):
    copies = [pltpu.make_async_copy(src, dst, sems.at[i]) for i, (src, dst) in enumerate(pairs)]
    for copy in copies:
        copy.start()
    return copies


def summary_kernel(unknowns, inc_hbm, dec_hbm, fw_hbm, con_hbm, ysend_ref, packed_ref, *refs):
    inc_out = refs[:unknowns]
    face_out = refs[unknowns:-5]
    inc_ref, dec_ref, fw_ref, con_ref, sems = refs[-5:]
    _, layers, rows, cols = inc_ref.shape
    copies = fetch([(inc_hbm, inc_ref), (dec_hbm, dec_ref), (fw_hbm, fw_ref), (con_hbm, con_ref)], sems)
    ysend_ref[...] = jnp.zeros(ysend_ref.shape, F32)
    for copy in copies:
        copy.wait()
    product = dec_ref[:, 0, :]
    value = inc_ref[:, 0, 0, :]
    for y in range(1, rows):
        decay = dec_ref[:, y, :]
        product = product * decay
        value = value * decay + inc_ref[:, 0, y, :]
    pair = lax.broadcasted_iota(jnp.int32, (rows, cols), 1) >> 1
    row = lax.broadcasted_iota(jnp.int32, (rows, cols), 0)
    packed = jnp.zeros((rows, cols), F32)
    planes = unknowns * layers
    for p in range(planes):
        packed = jnp.where(pair == p, pltpu.roll(inc_ref[p // layers, p % layers], 2 * p + 1, 1), packed)
    faces = [[fw_ref[d, l] * con_ref[d, l].astype(F32) for l in range(layers)] for d in range(3)]
    for layer in range(layers):
        p = planes + layer
        packed = jnp.where(pair == p, pltpu.roll(faces[0][layer], 2 * p + 1, 1), packed)
    ysend_ref[0, 0:unknowns] = product
    ysend_ref[1, 0:unknowns] = value
    for layer in range(layers):
        ysend_ref[2 + layer, 0:unknowns] = inc_ref[:, layer, 0, :]
        ysend_ref[2 + layers + layer, 0:unknowns] = inc_ref[:, layer, rows - 1, :]
        ysend_ref[2 + layers + layer, unknowns:unknowns + 1] = faces[1][layer][rows - 1:]
        face_out[layer][...] = faces[0][layer]
        face_out[layers + layer][...] = jnp.where(row == rows - 1, 0.0, faces[1][layer])
        face_out[2 * layers + layer][...] = faces[2][layer]
    packed_ref[...] = packed
    for u in range(unknowns):
        inc_out[u][...] = inc_ref[u]


def river_rows(xsend_ref, rows, at, value):
    for c in range(value.shape[1] // LANES):
        xsend_ref[pl.ds(rows + at + c, 1), :] = value[:, c * LANES:(c + 1) * LANES]


def river_kernel(pad, reach_local, code_ref, outflow_ref, inflow_ref, storage_ref, packed_ref, inc_ref, _, xsend_ref):
    layers, rows, cols = inc_ref.shape
    slots = code_ref.shape[2]
    wide = slots // LANES
    code = code_ref[0].astype(jnp.int32)
    reaches = code >> log2(rows * cols)
    cells = code & (rows * cols - 1)
    xsend_ref[rows:, :] = jnp.zeros((xsend_ref.shape[0] - rows, LANES), F32)
    xsend_ref[0:rows, :] = packed_ref[...]
    river_rows(xsend_ref, rows, 2 * pad, cells.astype(F32))
    river_rows(xsend_ref, rows, 2 * pad + wide, reaches.astype(F32))
    river_rows(xsend_ref, rows, 2 * pad + 2 * wide, outflow_ref[0])
    y_hot = hot(cells >> log2(cols), rows).astype(F32)
    y_hot3 = jnp.concatenate([y_hot, y_hot, y_hot], 0).astype(BF16)
    parts = jnp.concatenate(split3(inc_ref[0]), 0).astype(BF16)
    picked = lax.dot_general(parts, y_hot3, (((0,), (0,)), ((), ())), preferred_element_type=F32)
    values = jnp.sum(jnp.where(hot(cells & (cols - 1), cols), picked, 0.0), 0, keepdims=True)
    terms = stack3(inflow_ref[0] * values, 16)
    x_index = lax.axis_index("tx")
    owner = lax.broadcasted_iota(jnp.int32, (1, LANES), 1)
    stored = jnp.concatenate([storage_ref[0, :, 0:reach_local]] * (LANES // reach_local), 1)
    for c in range(reach_local * lax.axis_size("tx") // LANES):
        r_hot = hot(reaches, LANES, c * LANES).astype(F32).astype(BF16)
        total = lax.dot_general(terms, r_hot, (((1,), (1,)), ((), ())), preferred_element_type=F32)
        xsend_ref[pl.ds(rows + c, 1), :] = jnp.sum(total, 0, keepdims=True)
        xsend_ref[pl.ds(rows + pad + c, 1), :] = jnp.where(
            (owner + c * LANES) // reach_local == x_index, stored, 0.0
        )


def prefix_step(k, received, prior):
    upper = bit_of("ty", k) == 1
    if prior is None:
        return jnp.where(upper, received[0], 1.0), jnp.where(upper, received[1], 0.0)
    product = jnp.where(upper, prior[0] * received[0], prior[0])
    value = jnp.where(upper, prior[0] * received[1] + prior[1], prior[1])
    return product, value


def between_kernel(k, layers, sent_ref, got_ref, *refs):
    prior_ref = refs[0] if k > 0 else None
    send_ref, next_ref = refs[-2:]
    upper = bit_of("ty", k) == 1
    product, value = prefix_step(k, got_ref, prior_ref)
    next_ref[0] = product
    next_ref[1] = value
    own_a, own_b, got_a, got_b = sent_ref[0], sent_ref[1], got_ref[0], got_ref[1]
    low_b = jnp.where(upper, got_b, own_b)
    up_a = jnp.where(upper, own_a, got_a)
    up_b = jnp.where(upper, own_b, got_b)
    lead = send_ref.shape[0] - layers
    send_ref[lead - 1] = up_a * low_b + up_b
    if lead == 2:
        send_ref[0] = own_a * got_a
    for layer in range(layers):
        passed = got_ref[2 + layer]
        if k == 0:
            passed = jnp.where(upper, passed, got_ref[2 + layers + layer])
        send_ref[lead + layer] = passed


def beside_x(received, rows):
    index = lax.axis_index("tx")
    below = jnp.zeros((rows, LANES), F32)
    above = below
    for k, buffer in enumerate(received):
        low = (1 << k) - 1
        full = (2 << k) - 1
        above = jnp.where((index & full) == low, buffer[0:rows, :], above)
        below = jnp.where((index & full) == low + 1, buffer[0:rows, :], below)
    return below, above


def multiply(u, blocks, inc_refs, total):
    for j in range(len(inc_refs)):
        total = total + blocks[j].astype(F32) * inc_refs[j][...]
    return total


def ahead_kernel(unknowns, count, blocks_hbm, dec_hbm, *refs):
    inc_refs, refs = refs[2:2 + unknowns], refs[2 + unknowns:]
    out_refs, refs = refs[:unknowns], refs[unknowns:]
    grown_refs, refs = refs[:unknowns], refs[unknowns:]
    blocks_ref, top_ref, dec_ref, value_ref, product_ref, sems = refs
    _, rows, cols = top_ref.shape
    copies = fetch(
        [(dec_hbm, dec_ref)] + [(blocks_hbm.at[i], blocks_ref.at[i]) for i in range(count)], sems
    )
    for u in range(unknowns):
        top_ref[u] = inc_refs[u][0]
    copies[0].wait()
    product = 0.1 * dec_ref[:, 0, :]
    value = 0.1 * top_ref[:, 0, :]
    product_ref[:, 0, :] = product
    value_ref[:, 0, :] = value
    for y in range(1, rows):
        decay = dec_ref[:, y, :]
        product = product * decay
        value = value * decay + 0.1 * top_ref[:, y, :]
        product_ref[:, y, :] = product
        value_ref[:, y, :] = value
    for u in range(unknowns):
        grown_refs[u][...] = product_ref[u]
        if u >= count:
            out_refs[u][...] = value_ref[u]
            continue
        if u % WAITS == 0:
            for copy in copies[1 + u:1 + min(u + WAITS, count)]:
                copy.wait()
        total = multiply(u, blocks_ref.at[u], inc_refs, jnp.zeros(out_refs[u].shape, F32))
        out_refs[u][0] = total[0] + value_ref[u]
        out_refs[u][1:] = total[1:]


def local_kernel(x_rounds, pad, reach_rows, slots, unknowns, layers, count, blocks_hbm, sent_ref, *refs):
    received, refs = refs[:x_rounds], refs[x_rounds:]
    inc_refs, refs = refs[:unknowns], refs[unknowns:]
    face_refs, refs = refs[:3 * layers], refs[3 * layers:]
    done_refs, refs = refs[:unknowns], refs[unknowns:]
    out_refs, refs = refs[:unknowns], refs[unknowns:]
    blocks_ref, flux_ref, sems = refs
    _, rows, cols = inc_refs[0].shape
    copies = fetch(
        [(blocks_hbm.at[i], blocks_ref.at[i - count]) for i in range(count, unknowns)],
        sems,
    )
    lane = lax.broadcasted_iota(jnp.int32, (rows, cols), 1)
    wide = slots // LANES

    def slot_row(at):
        start = rows + 2 * pad + at * wide
        return jnp.concatenate([sent_ref[start + c:start + c + 1, :] for c in range(wide)], 1)

    cells = slot_row(0).astype(jnp.int32)
    reaches = slot_row(1).astype(jnp.int32)
    totals = sent_ref[rows:rows + pad, :] + received[-1][rows:rows + pad, :]
    storage = sent_ref[rows + pad:rows + 2 * pad, :] + received[-1][rows + pad:rows + 2 * pad, :]
    shift = log2(cols)
    picked = jnp.zeros((16, slots), F32)
    for c in range(reach_rows):
        section = stack3(totals[c:c + 1] / storage[c:c + 1], 16)
        r_hot = hot(reaches, LANES, c * LANES).astype(F32).astype(BF16)
        picked = picked + lax.dot_general(section, r_hot, (((1,), (0,)), ((), ())), preferred_element_type=F32)
    back = slot_row(2) * jnp.sum(picked, 0, keepdims=True)
    y_hot = hot(cells >> shift, rows)
    spread = jnp.concatenate([jnp.where(y_hot, part, 0.0) for part in split3(back)], 0).astype(BF16)
    x_hot = hot(cells & (cols - 1), cols).astype(F32).astype(BF16)
    added = lax.dot_general(spread, x_hot, (((1,), (1,)), ((), ())), preferred_element_type=F32)
    river = added[0:rows] + added[rows:2 * rows] + added[2 * rows:3 * rows]
    left, right = beside_x(received, rows)
    rim = jnp.where(lane & 1 == 0, pltpu.roll(right, cols - 1, 1), pltpu.roll(left, 1, 1))
    planes = unknowns * layers
    for layer in range(layers):
        face_x = face_refs[layer][...]
        face_y = face_refs[layers + layer][...]
        face_z = face_refs[2 * layers + layer][...]
        face_left = pltpu.roll(rim, (cols - 1 - 2 * (planes + layer)) % cols, 1)
        for first in range(0, unknowns, GROUP):
            group = range(first, min(first + GROUP, unknowns))
            here = jnp.stack([inc_refs[u][layer] for u in group])
            beside = jnp.stack([pltpu.roll(rim, cols - 1 - 2 * (u * layers + layer), 1) for u in group])
            flow_x = face_x * (here - jnp.where(lane == cols - 1, beside, pltpu.roll(here, cols - 1, 2)))
            from_left = jnp.where(lane == 0, face_left * (beside - here), pltpu.roll(flow_x, 1, 2))
            flow_y = face_y * (here - pltpu.roll(here, rows - 1, 1))
            total = flow_x - from_left + (flow_y - pltpu.roll(flow_y, 1, 1))
            if layer + 1 < layers:
                total = total + face_z * (here - jnp.stack([inc_refs[u][layer + 1] for u in group]))
            else:
                total = total + face_z * here
            if layer > 0:
                over = jnp.stack([inc_refs[u][layer - 1] for u in group])
                total = total + face_refs[2 * layers + layer - 1][...] * (here - over)
            for u in group:
                flux_ref[u, layer] = total[u - first] + river if u + layer == 0 else total[u - first]
    for u in range(unknowns):
        total = flux_ref[u]
        if u < count:
            out_refs[u][...] = total + done_refs[u][...]
            continue
        at = u - count
        if at % WAITS == 0:
            for copy in copies[at:at + WAITS]:
                copy.wait()
        total = multiply(u, blocks_ref.at[at], inc_refs, total)
        out_refs[u][0] = total[0] + done_refs[u][...]
        out_refs[u][1:] = total[1:]


def final_kernel(unknowns, y_rounds, *refs):
    part_refs = refs[:unknowns]
    grown_refs = refs[unknowns:2 * unknowns]
    own_ref = refs[2 * unknowns]
    got = refs[2 * unknowns + 1:2 * unknowns + 1 + y_rounds]
    prior_ref, out_ref = refs[-2:]
    layers, rows, cols = part_refs[0].shape
    upper = bit_of("ty", y_rounds - 1) == 1
    carry = jnp.where(upper, prior_ref[0] * got[-1][0] + prior_ref[1], prior_ref[1])
    index = lax.axis_index("ty")
    odd = (index & 1) == 1
    at = lax.broadcasted_iota(jnp.int32, (8, cols), 0)
    starts = []
    ends = []
    for layer in range(layers):
        passed_up = jnp.zeros(carry.shape, F32)
        passed_down = passed_up
        for k in range(1, y_rounds):
            full = (2 << k) - 1
            passed_up = jnp.where((index & full) == (1 << k), got[k][got[k].shape[0] - layers + layer], passed_up)
            passed_down = jnp.where((index & full) == (1 << k) - 1, got[k][got[k].shape[0] - layers + layer], passed_down)
        below = jnp.where(odd, got[0][2 + layers + layer], passed_up)
        above = jnp.where(odd, passed_down, got[0][2 + layer])
        low_face = below[unknowns:unknowns + 1]
        top_face = own_ref[2 + layers + layer, unknowns:unknowns + 1]
        starts.append(low_face * (own_ref[2 + layer] - below))
        ends.append(top_face * (own_ref[2 + layers + layer] - above))
    for u in range(unknowns):
        for layer in range(layers):
            total = part_refs[u][layer]
            if layer == 0:
                total = total + grown_refs[u][...] * carry[u:u + 1]
            head = total[0:8] + jnp.where(at == 0, starts[layer][u:u + 1], 0.0)
            foot = total[rows - 8:rows] + jnp.where(at == 7, ends[layer][u:u + 1], 0.0)
            out_ref[u, layer, 0:8, :] = head
            out_ref[u, layer, 8:rows - 8, :] = total[8:rows - 8]
            out_ref[u, layer, rows - 8:rows, :] = foot


def call(kernel, outs, args, far=0, scratch=(), grant=32 * 1024, cost=0):
    vmem = pl.BlockSpec(memory_space=pltpu.VMEM)
    hbm = pl.BlockSpec(memory_space=pltpu.HBM)
    return pl.pallas_call(
        kernel,
        out_shape=[jax.ShapeDtypeStruct(o.shape, o.dtype) for o in outs],
        in_specs=[hbm] * far + [vmem] * (len(args) - far),
        out_specs=[vmem] * len(outs),
        scratch_shapes=list(scratch),
        compiler_params=pltpu.CompilerParams(vmem_limit_bytes=grant * 1024),
        cost_estimate=pl.CostEstimate(flops=0, bytes_accessed=cost, transcendentals=0),
    )(*args)


def f32(*shape):
    return jax.ShapeDtypeStruct(shape, F32)


def like(a, *shape):
    return pltpu.VMEM(shape or a.shape, a.dtype)


SUMMARY_GRANT = 54600
LOCAL_GRANT = 52000
LOCAL_COST = 0
RIVER_COST = 0
GROUP = 13
WAITS = 2
AHEAD = 4
EXTRA = 0
AHEAD_GRANT = 54080


def body(
    increment,
    blocks,
    face_weights,
    connected,
    overland_decay,
    river_cell,
    river_reach,
    river_count,
    inflow,
    outflow,
    storage,
):
    unknowns, layers, rows, cols = increment.shape
    x_size = lax.axis_size("tx")
    y_size = lax.axis_size("ty")
    x_rounds = log2(x_size)
    y_rounds = log2(y_size)
    slots = river_cell.shape[2]
    decay = jnp.swapaxes(overland_decay, 1, 2)
    reach_rows = storage.shape[1] * x_size // LANES
    pad = -(-reach_rows // 8) * 8
    tall = -(-(unknowns + 1) // 8) * 8
    plane = f32(rows, cols)
    y_first, packed, *kept = call(
        functools.partial(summary_kernel, unknowns),
        [f32(2 + 2 * layers, tall, cols), plane] + [f32(layers, rows, cols)] * unknowns + [plane] * (3 * layers),
        [increment, decay, face_weights, connected],
        far=4,
        scratch=[
            like(increment), like(decay), like(face_weights), like(connected), pltpu.SemaphoreType.DMA((4,)),
        ],
        grant=SUMMARY_GRANT,
    )
    live = lax.broadcasted_iota(jnp.int32, river_cell.shape, 2) < river_count[:, :, None]
    code = jnp.where(live, (river_cell + (rows * cols) * river_reach).astype(F32), 0.0)
    reach_local = storage.shape[1]
    stored = jnp.pad(storage[None], ((0, 0), (0, 0), (0, slots - reach_local)))
    stored = jnp.where(lax.broadcasted_iota(jnp.int32, stored.shape, 2) < reach_local, stored, jnp.where(live, 1.0, 0.0))
    (x_send,) = call(
        functools.partial(river_kernel, pad, reach_local),
        [f32(EXTRA + rows + 2 * pad + -(-3 * slots // LANES // 8) * 8, cols)],
        [code, jnp.where(live, outflow, 0.0), jnp.where(live, inflow, 0.0), stored, packed, kept[0], y_first],
        cost=RIVER_COST,
    )
    y_send = y_first
    y_got = []
    x_got = []
    prior = None
    at = lax.broadcasted_iota(jnp.int32, x_send.shape, 0)
    summed = (at >= rows) & (at < rows + 2 * pad)
    for k in range(max(x_rounds, y_rounds)):
        if k < y_rounds:
            y_got.append(lax.ppermute(y_send, "ty", [(i, i ^ (1 << k)) for i in range(y_size)]))
        if k < x_rounds:
            x_got.append(lax.ppermute(x_send, "tx", [(i, i ^ ((2 << k) - 1)) for i in range(x_size)]))
            if k + 1 < x_rounds:
                x_send = x_send + jnp.where(summed, x_got[-1], 0.0)
        if k + 1 < y_rounds:
            y_send, prior = call(
                functools.partial(between_kernel, k, layers),
                [f32((2 if k + 2 < y_rounds else 1) + layers, tall, cols), f32(2, tall, cols)],
                [y_send, y_got[-1]] + ([prior] + list(ahead[:1]) if k > 0 else []),
            )
            if k == 0:
                made = call(
                    functools.partial(ahead_kernel, unknowns, AHEAD),
                    [f32(layers, rows, cols)] * AHEAD + [plane] * (2 * unknowns - AHEAD),
                    [blocks, decay, y_send, x_send, *kept[:unknowns]],
                    far=2,
                    scratch=[
                        like(blocks, AHEAD, *blocks.shape[1:]), like(decay), like(decay), like(decay), like(decay),
                        pltpu.SemaphoreType.DMA((1 + AHEAD,)),
                    ],
                    grant=AHEAD_GRANT,
                )
                ahead, grown = made[:unknowns], made[unknowns:]
    local = call(
        functools.partial(local_kernel, x_rounds, pad, reach_rows, slots, unknowns, layers, AHEAD),
        [f32(layers, rows, cols)] * unknowns,
        [blocks, x_send, *x_got, *kept, *ahead],
        far=1,
        scratch=[
            like(blocks, unknowns - AHEAD, *blocks.shape[1:]), like(increment),
            pltpu.SemaphoreType.DMA((unknowns - AHEAD,)),
        ],
        grant=LOCAL_GRANT,
        cost=LOCAL_COST,
    )
    (total,) = call(
        functools.partial(final_kernel, unknowns, y_rounds),
        [increment],
        [*local, *grown, y_first, *y_got, prior],
    )
    return total


def solution(mesh):
    in_specs = (
        P(None, None, "ty", "tx"),
        P(None, None, None, "ty", "tx"),
        P(None, None, "ty", "tx"),
        P(None, None, "ty", "tx"),
        P(None, "tx", "ty"),
        P("tx", "ty", None),
        P("tx", "ty", None),
        P("tx", "ty"),
        P("tx", "ty", None),
        P("tx", "ty", None),
        P("ty", "tx"),
    )
    out_specs = P(None, None, "ty", "tx")
    return jax.shard_map(body, mesh=mesh, in_specs=in_specs, out_specs=out_specs, check_vma=False)
```

```python
import functools
import jax
import jax.numpy as jnp
from jax import lax
from jax.experimental import pallas as pl
from jax.experimental.pallas import tpu as pltpu
from jax.sharding import PartitionSpec as P

F32 = jnp.float32
BF16 = jnp.bfloat16
LANES = 128


def log2(n):
    return n.bit_length() - 1


def bit_of(axis, k):
    return (lax.axis_index(axis) >> k) & 1


def split3(x):
    hi = x.astype(BF16).astype(F32)
    rest = x - hi
    mid = rest.astype(BF16).astype(F32)
    return hi, mid, rest - mid


def stack3(row, height):
    hi, mid, lo = split3(row)
    at = lax.broadcasted_iota(jnp.int32, (height, row.shape[1]), 0)
    zero = jnp.zeros((height, row.shape[1]), F32)
    out = jnp.where(at == 0, hi, jnp.where(at == 1, mid, jnp.where(at == 2, lo, zero)))
    return out.astype(BF16)


def hot(index_row, size, start=0):
    at = lax.broadcasted_iota(jnp.int32, (size, index_row.shape[1]), 0) + start
    return at == index_row


def fetch(pairs, sems):
    copies = [pltpu.make_async_copy(src, dst, sems.at[i]) for i, (src, dst) in enumerate(pairs)]
    for copy in copies:
        copy.start()
    return copies


def summary_kernel(unknowns, inc_hbm, dec_hbm, fw_hbm, con_hbm, ysend_ref, packed_ref, *refs):
    inc_out = refs[:unknowns]
    face_out = refs[unknowns:-5]
    inc_ref, dec_ref, fw_ref, con_ref, sems = refs[-5:]
    _, layers, rows, cols = inc_ref.shape
    copies = fetch([(inc_hbm, inc_ref), (dec_hbm, dec_ref), (fw_hbm, fw_ref), (con_hbm, con_ref)], sems)
    ysend_ref[...] = jnp.zeros(ysend_ref.shape, F32)
    for copy in copies:
        copy.wait()
    product = dec_ref[:, 0, :]
    value = inc_ref[:, 0, 0, :]
    for y in range(1, rows):
        decay = dec_ref[:, y, :]
        product = product * decay
        value = value * decay + inc_ref[:, 0, y, :]
    pair = lax.broadcasted_iota(jnp.int32, (rows, cols), 1) >> 1
    row = lax.broadcasted_iota(jnp.int32, (rows, cols), 0)
    packed = jnp.zeros((rows, cols), F32)
    planes = unknowns * layers
    for p in range(planes):
        packed = jnp.where(pair == p, pltpu.roll(inc_ref[p // layers, p % layers], 2 * p + 1, 1), packed)
    faces = [[fw_ref[d, l] * con_ref[d, l].astype(F32) for l in range(layers)] for d in range(3)]
    for layer in range(layers):
        p = planes + layer
        packed = jnp.where(pair == p, pltpu.roll(faces[0][layer], 2 * p + 1, 1), packed)
    ysend_ref[0, 0:unknowns] = product
    ysend_ref[1, 0:unknowns] = value
    for layer in range(layers):
        ysend_ref[2 + layer, 0:unknowns] = inc_ref[:, layer, 0, :]
        ysend_ref[2 + layers + layer, 0:unknowns] = inc_ref[:, layer, rows - 1, :]
        ysend_ref[2 + layers + layer, unknowns:unknowns + 1] = faces[1][layer][rows - 1:]
        face_out[layer][...] = faces[0][layer]
        face_out[layers + layer][...] = jnp.where(row == rows - 1, 0.0, faces[1][layer])
        face_out[2 * layers + layer][...] = faces[2][layer]
    packed_ref[...] = packed
    for u in range(unknowns):
        inc_out[u][...] = inc_ref[u]


def river_rows(xsend_ref, rows, at, value):
    for c in range(value.shape[1] // LANES):
        xsend_ref[pl.ds(rows + at + c, 1), :] = value[:, c * LANES:(c + 1) * LANES]


def river_kernel(pad, reach_local, code_ref, outflow_ref, inflow_ref, storage_ref, packed_ref, inc_ref, _, xsend_ref):
    layers, rows, cols = inc_ref.shape
    slots = code_ref.shape[2]
    wide = slots // LANES
    code = code_ref[0].astype(jnp.int32)
    reaches = code >> log2(rows * cols)
    cells = code & (rows * cols - 1)
    xsend_ref[rows:, :] = jnp.zeros((xsend_ref.shape[0] - rows, LANES), F32)
    xsend_ref[0:rows, :] = packed_ref[...]
    river_rows(xsend_ref, rows, 2 * pad, cells.astype(F32))
    river_rows(xsend_ref, rows, 2 * pad + wide, reaches.astype(F32))
    river_rows(xsend_ref, rows, 2 * pad + 2 * wide, outflow_ref[0])
    y_hot = hot(cells >> log2(cols), rows).astype(F32)
    y_hot3 = jnp.concatenate([y_hot, y_hot, y_hot], 0).astype(BF16)
    parts = jnp.concatenate(split3(inc_ref[0]), 0).astype(BF16)
    picked = lax.dot_general(parts, y_hot3, (((0,), (0,)), ((), ())), preferred_element_type=F32)
    values = jnp.sum(jnp.where(hot(cells & (cols - 1), cols), picked, 0.0), 0, keepdims=True)
    terms = stack3(inflow_ref[0] * values, 16)
    x_index = lax.axis_index("tx")
    owner = lax.broadcasted_iota(jnp.int32, (1, LANES), 1)
    stored = jnp.concatenate([storage_ref[0, :, 0:reach_local]] * (LANES // reach_local), 1)
    for c in range(reach_local * lax.axis_size("tx") // LANES):
        r_hot = hot(reaches, LANES, c * LANES).astype(F32).astype(BF16)
        total = lax.dot_general(terms, r_hot, (((1,), (1,)), ((), ())), preferred_element_type=F32)
        xsend_ref[pl.ds(rows + c, 1), :] = jnp.sum(total, 0, keepdims=True)
        xsend_ref[pl.ds(rows + pad + c, 1), :] = jnp.where(
            (owner + c * LANES) // reach_local == x_index, stored, 0.0
        )


def prefix_step(k, received, prior):
    upper = bit_of("ty", k) == 1
    if prior is None:
        return jnp.where(upper, received[0], 1.0), jnp.where(upper, received[1], 0.0)
    product = jnp.where(upper, prior[0] * received[0], prior[0])
    value = jnp.where(upper, prior[0] * received[1] + prior[1], prior[1])
    return product, value


def between_kernel(k, layers, sent_ref, got_ref, *refs):
    prior_ref = refs[0] if k > 0 else None
    send_ref, next_ref = refs[-2:]
    upper = bit_of("ty", k) == 1
    product, value = prefix_step(k, got_ref, prior_ref)
    next_ref[0] = product
    next_ref[1] = value
    own_a, own_b, got_a, got_b = sent_ref[0], sent_ref[1], got_ref[0], got_ref[1]
    low_b = jnp.where(upper, got_b, own_b)
    up_a = jnp.where(upper, own_a, got_a)
    up_b = jnp.where(upper, own_b, got_b)
    lead = send_ref.shape[0] - layers
    send_ref[lead - 1] = up_a * low_b + up_b
    if lead == 2:
        send_ref[0] = own_a * got_a
    for layer in range(layers):
        passed = got_ref[2 + layer]
        if k == 0:
            passed = jnp.where(upper, passed, got_ref[2 + layers + layer])
        send_ref[lead + layer] = passed


def beside_x(received, rows):
    index = lax.axis_index("tx")
    below = jnp.zeros((rows, LANES), F32)
    above = below
    for k, buffer in enumerate(received):
        low = (1 << k) - 1
        full = (2 << k) - 1
        above = jnp.where((index & full) == low, buffer[0:rows, :], above)
        below = jnp.where((index & full) == low + 1, buffer[0:rows, :], below)
    return below, above


def multiply(u, blocks, inc_refs, total):
    for j in range(len(inc_refs)):
        total = total + blocks[j].astype(F32) * inc_refs[j][...]
    return total


def ahead_kernel(unknowns, count, blocks_hbm, dec_hbm, *refs):
    inc_refs, refs = refs[2:2 + unknowns], refs[2 + unknowns:]
    out_refs, refs = refs[:unknowns], refs[unknowns:]
    grown_refs, refs = refs[:unknowns], refs[unknowns:]
    blocks_ref, top_ref, dec_ref, value_ref, product_ref, sems = refs
    _, rows, cols = top_ref.shape
    copies = fetch(
        [(dec_hbm, dec_ref)] + [(blocks_hbm.at[i], blocks_ref.at[i]) for i in range(count)], sems
    )
    for u in range(unknowns):
        top_ref[u] = inc_refs[u][0]
    copies[0].wait()
    product = 0.1 * dec_ref[:, 0, :]
    value = 0.1 * top_ref[:, 0, :]
    product_ref[:, 0, :] = product
    value_ref[:, 0, :] = value
    for y in range(1, rows):
        decay = dec_ref[:, y, :]
        product = product * decay
        value = value * decay + 0.1 * top_ref[:, y, :]
        product_ref[:, y, :] = product
        value_ref[:, y, :] = value
    for u in range(unknowns):
        grown_refs[u][...] = product_ref[u]
        if u >= count:
            out_refs[u][...] = value_ref[u]
            continue
        if u % WAITS == 0:
            for copy in copies[1 + u:1 + min(u + WAITS, count)]:
                copy.wait()
        total = multiply(u, blocks_ref.at[u], inc_refs, jnp.zeros(out_refs[u].shape, F32))
        out_refs[u][0] = total[0] + value_ref[u]
        out_refs[u][1:] = total[1:]


def local_kernel(x_rounds, pad, reach_rows, slots, unknowns, layers, count, blocks_hbm, sent_ref, *refs):
    received, refs = refs[:x_rounds], refs[x_rounds:]
    inc_refs, refs = refs[:unknowns], refs[unknowns:]
    face_refs, refs = refs[:3 * layers], refs[3 * layers:]
    done_refs, refs = refs[:unknowns], refs[unknowns:]
    out_refs, refs = refs[:unknowns], refs[unknowns:]
    blocks_ref, flux_ref, sems = refs
    _, rows, cols = inc_refs[0].shape
    copies = fetch(
        [(blocks_hbm.at[i], blocks_ref.at[i - count]) for i in range(count, unknowns)],
        sems,
    )
    lane = lax.broadcasted_iota(jnp.int32, (rows, cols), 1)
    wide = slots // LANES

    def slot_row(at):
        start = rows + 2 * pad + at * wide
        return jnp.concatenate([sent_ref[start + c:start + c + 1, :] for c in range(wide)], 1)

    cells = slot_row(0).astype(jnp.int32)
    reaches = slot_row(1).astype(jnp.int32)
    totals = sent_ref[rows:rows + pad, :] + received[-1][rows:rows + pad, :]
    storage = sent_ref[rows + pad:rows + 2 * pad, :] + received[-1][rows + pad:rows + 2 * pad, :]
    shift = log2(cols)
    picked = jnp.zeros((16, slots), F32)
    for c in range(reach_rows):
        section = stack3(totals[c:c + 1] / storage[c:c + 1], 16)
        r_hot = hot(reaches, LANES, c * LANES).astype(F32).astype(BF16)
        picked = picked + lax.dot_general(section, r_hot, (((1,), (0,)), ((), ())), preferred_element_type=F32)
    back = slot_row(2) * jnp.sum(picked, 0, keepdims=True)
    y_hot = hot(cells >> shift, rows)
    spread = jnp.concatenate([jnp.where(y_hot, part, 0.0) for part in split3(back)], 0).astype(BF16)
    x_hot = hot(cells & (cols - 1), cols).astype(F32).astype(BF16)
    added = lax.dot_general(spread, x_hot, (((1,), (1,)), ((), ())), preferred_element_type=F32)
    river = added[0:rows] + added[rows:2 * rows] + added[2 * rows:3 * rows]
    left, right = beside_x(received, rows)
    rim = jnp.where(lane & 1 == 0, pltpu.roll(right, cols - 1, 1), pltpu.roll(left, 1, 1))
    planes = unknowns * layers
    for layer in range(layers):
        face_x = face_refs[layer][...]
        face_y = face_refs[layers + layer][...]
        face_z = face_refs[2 * layers + layer][...]
        face_left = pltpu.roll(rim, (cols - 1 - 2 * (planes + layer)) % cols, 1)
        for first in range(0, unknowns, GROUP):
            group = range(first, min(first + GROUP, unknowns))
            here = jnp.stack([inc_refs[u][layer] for u in group])
            beside = jnp.stack([pltpu.roll(rim, cols - 1 - 2 * (u * layers + layer), 1) for u in group])
            flow_x = face_x * (here - jnp.where(lane == cols - 1, beside, pltpu.roll(here, cols - 1, 2)))
            from_left = jnp.where(lane == 0, face_left * (beside - here), pltpu.roll(flow_x, 1, 2))
            flow_y = face_y * (here - pltpu.roll(here, rows - 1, 1))
            total = flow_x - from_left + (flow_y - pltpu.roll(flow_y, 1, 1))
            if layer + 1 < layers:
                total = total + face_z * (here - jnp.stack([inc_refs[u][layer + 1] for u in group]))
            else:
                total = total + face_z * here
            if layer > 0:
                over = jnp.stack([inc_refs[u][layer - 1] for u in group])
                total = total + face_refs[2 * layers + layer - 1][...] * (here - over)
            for u in group:
                flux_ref[u, layer] = total[u - first]
    for u in [*range(1, unknowns), 0]:
        total = flux_ref[u]
        if u < count:
            total = total + done_refs[u][...]
            if u == 0:
                out_refs[u][0] = total[0] + river
                out_refs[u][1:] = total[1:]
            else:
                out_refs[u][...] = total
            continue
        at = u - count
        if at % WAITS == 0:
            for copy in copies[at:at + WAITS]:
                copy.wait()
        total = multiply(u, blocks_ref.at[at], inc_refs, total)
        out_refs[u][0] = total[0] + done_refs[u][...]
        out_refs[u][1:] = total[1:]


def final_kernel(unknowns, y_rounds, *refs):
    part_refs = refs[:unknowns]
    grown_refs = refs[unknowns:2 * unknowns]
    own_ref = refs[2 * unknowns]
    got = refs[2 * unknowns + 1:2 * unknowns + 1 + y_rounds]
    prior_ref, out_ref = refs[-2:]
    layers, rows, cols = part_refs[0].shape
    upper = bit_of("ty", y_rounds - 1) == 1
    carry = jnp.where(upper, prior_ref[0] * got[-1][0] + prior_ref[1], prior_ref[1])
    index = lax.axis_index("ty")
    odd = (index & 1) == 1
    at = lax.broadcasted_iota(jnp.int32, (8, cols), 0)
    starts = []
    ends = []
    for layer in range(layers):
        passed_up = jnp.zeros(carry.shape, F32)
        passed_down = passed_up
        for k in range(1, y_rounds):
            full = (2 << k) - 1
            passed_up = jnp.where((index & full) == (1 << k), got[k][got[k].shape[0] - layers + layer], passed_up)
            passed_down = jnp.where((index & full) == (1 << k) - 1, got[k][got[k].shape[0] - layers + layer], passed_down)
        below = jnp.where(odd, got[0][2 + layers + layer], passed_up)
        above = jnp.where(odd, passed_down, got[0][2 + layer])
        low_face = below[unknowns:unknowns + 1]
        top_face = own_ref[2 + layers + layer, unknowns:unknowns + 1]
        starts.append(low_face * (own_ref[2 + layer] - below))
        ends.append(top_face * (own_ref[2 + layers + layer] - above))
    for u in range(unknowns):
        for layer in range(layers):
            total = part_refs[u][layer]
            if layer == 0:
                total = total + grown_refs[u][...] * carry[u:u + 1]
            head = total[0:8] + jnp.where(at == 0, starts[layer][u:u + 1], 0.0)
            foot = total[rows - 8:rows] + jnp.where(at == 7, ends[layer][u:u + 1], 0.0)
            out_ref[u, layer, 0:8, :] = head
            out_ref[u, layer, 8:rows - 8, :] = total[8:rows - 8]
            out_ref[u, layer, rows - 8:rows, :] = foot


def call(kernel, outs, args, far=0, scratch=(), grant=32 * 1024, cost=0):
    vmem = pl.BlockSpec(memory_space=pltpu.VMEM)
    hbm = pl.BlockSpec(memory_space=pltpu.HBM)
    return pl.pallas_call(
        kernel,
        out_shape=[jax.ShapeDtypeStruct(o.shape, o.dtype) for o in outs],
        in_specs=[hbm] * far + [vmem] * (len(args) - far),
        out_specs=[vmem] * len(outs),
        scratch_shapes=list(scratch),
        compiler_params=pltpu.CompilerParams(vmem_limit_bytes=grant * 1024),
        cost_estimate=pl.CostEstimate(flops=0, bytes_accessed=cost, transcendentals=0),
    )(*args)


def f32(*shape):
    return jax.ShapeDtypeStruct(shape, F32)


def like(a, *shape):
    return pltpu.VMEM(shape or a.shape, a.dtype)


SUMMARY_GRANT = 54600
LOCAL_GRANT = 52000
LOCAL_COST = 0
RIVER_COST = 0
GROUP = 13
WAITS = 2
AHEAD = 4
EXTRA = 0
AHEAD_GRANT = 54080


def body(
    increment,
    blocks,
    face_weights,
    connected,
    overland_decay,
    river_cell,
    river_reach,
    river_count,
    inflow,
    outflow,
    storage,
):
    unknowns, layers, rows, cols = increment.shape
    x_size = lax.axis_size("tx")
    y_size = lax.axis_size("ty")
    x_rounds = log2(x_size)
    y_rounds = log2(y_size)
    slots = river_cell.shape[2]
    decay = jnp.swapaxes(overland_decay, 1, 2)
    reach_rows = storage.shape[1] * x_size // LANES
    pad = -(-reach_rows // 8) * 8
    tall = -(-(unknowns + 1) // 8) * 8
    plane = f32(rows, cols)
    y_first, packed, *kept = call(
        functools.partial(summary_kernel, unknowns),
        [f32(2 + 2 * layers, tall, cols), plane] + [f32(layers, rows, cols)] * unknowns + [plane] * (3 * layers),
        [increment, decay, face_weights, connected],
        far=4,
        scratch=[
            like(increment), like(decay), like(face_weights), like(connected), pltpu.SemaphoreType.DMA((4,)),
        ],
        grant=SUMMARY_GRANT,
    )
    live = lax.broadcasted_iota(jnp.int32, river_cell.shape, 2) < river_count[:, :, None]
    code = jnp.where(live, (river_cell + (rows * cols) * river_reach).astype(F32), 0.0)
    reach_local = storage.shape[1]
    stored = jnp.pad(storage[None], ((0, 0), (0, 0), (0, slots - reach_local)))
    stored = jnp.where(lax.broadcasted_iota(jnp.int32, stored.shape, 2) < reach_local, stored, jnp.where(live, 1.0, 0.0))
    (x_send,) = call(
        functools.partial(river_kernel, pad, reach_local),
        [f32(EXTRA + rows + 2 * pad + -(-3 * slots // LANES // 8) * 8, cols)],
        [code, jnp.where(live, outflow, 0.0), jnp.where(live, inflow, 0.0), stored, packed, kept[0], y_first],
        cost=RIVER_COST,
    )
    y_send = y_first
    y_got = []
    x_got = []
    prior = None
    at = lax.broadcasted_iota(jnp.int32, x_send.shape, 0)
    summed = (at >= rows) & (at < rows + 2 * pad)
    for k in range(max(x_rounds, y_rounds)):
        if k < y_rounds:
            y_got.append(lax.ppermute(y_send, "ty", [(i, i ^ (1 << k)) for i in range(y_size)]))
        if k < x_rounds:
            x_got.append(lax.ppermute(x_send, "tx", [(i, i ^ ((2 << k) - 1)) for i in range(x_size)]))
            if k + 1 < x_rounds:
                x_send = x_send + jnp.where(summed, x_got[-1], 0.0)
        if k + 1 < y_rounds:
            y_send, prior = call(
                functools.partial(between_kernel, k, layers),
                [f32((2 if k + 2 < y_rounds else 1) + layers, tall, cols), f32(2, tall, cols)],
                [y_send, y_got[-1]] + ([prior] + list(ahead[:1]) if k > 0 else []),
            )
            if k == 0:
                made = call(
                    functools.partial(ahead_kernel, unknowns, AHEAD),
                    [f32(layers, rows, cols)] * AHEAD + [plane] * (2 * unknowns - AHEAD),
                    [blocks, decay, y_send, x_send, *kept[:unknowns]],
                    far=2,
                    scratch=[
                        like(blocks, AHEAD, *blocks.shape[1:]), like(decay), like(decay), like(decay), like(decay),
                        pltpu.SemaphoreType.DMA((1 + AHEAD,)),
                    ],
                    grant=AHEAD_GRANT,
                )
                ahead, grown = made[:unknowns], made[unknowns:]
    local = call(
        functools.partial(local_kernel, x_rounds, pad, reach_rows, slots, unknowns, layers, AHEAD),
        [f32(layers, rows, cols)] * unknowns,
        [blocks, x_send, *x_got, *kept, *ahead],
        far=1,
        scratch=[
            like(blocks, unknowns - AHEAD, *blocks.shape[1:]), like(increment),
            pltpu.SemaphoreType.DMA((unknowns - AHEAD,)),
        ],
        grant=LOCAL_GRANT,
        cost=LOCAL_COST,
    )
    (total,) = call(
        functools.partial(final_kernel, unknowns, y_rounds),
        [increment],
        [*local, *grown, y_first, *y_got, prior],
    )
    return total


def solution(mesh):
    in_specs = (
        P(None, None, "ty", "tx"),
        P(None, None, None, "ty", "tx"),
        P(None, None, "ty", "tx"),
        P(None, None, "ty", "tx"),
        P(None, "tx", "ty"),
        P("tx", "ty", None),
        P("tx", "ty", None),
        P("tx", "ty"),
        P("tx", "ty", None),
        P("tx", "ty", None),
        P("ty", "tx"),
    )
    out_specs = P(None, None, "ty", "tx")
    return jax.shard_map(body, mesh=mesh, in_specs=in_specs, out_specs=out_specs, check_vma=False)
```

```python
import functools
import jax
import jax.numpy as jnp
from jax import lax
from jax.experimental import pallas as pl
from jax.experimental.pallas import tpu as pltpu
from jax.sharding import PartitionSpec as P

F32 = jnp.float32
BF16 = jnp.bfloat16
LANES = 128


def log2(n):
    return n.bit_length() - 1


def bit_of(axis, k):
    return (lax.axis_index(axis) >> k) & 1


def split3(x):
    hi = x.astype(BF16).astype(F32)
    rest = x - hi
    mid = rest.astype(BF16).astype(F32)
    return hi, mid, rest - mid


def stack3(row, height):
    hi, mid, lo = split3(row)
    at = lax.broadcasted_iota(jnp.int32, (height, row.shape[1]), 0)
    zero = jnp.zeros((height, row.shape[1]), F32)
    out = jnp.where(at == 0, hi, jnp.where(at == 1, mid, jnp.where(at == 2, lo, zero)))
    return out.astype(BF16)


def hot(index_row, size, start=0):
    at = lax.broadcasted_iota(jnp.int32, (size, index_row.shape[1]), 0) + start
    return at == index_row


def fetch(pairs, sems):
    copies = [pltpu.make_async_copy(src, dst, sems.at[i]) for i, (src, dst) in enumerate(pairs)]
    for copy in copies:
        copy.start()
    return copies


def summary_kernel(unknowns, inc_hbm, dec_hbm, fw_hbm, con_hbm, ysend_ref, packed_ref, *refs):
    inc_out = refs[:unknowns]
    face_out = refs[unknowns:-5]
    inc_ref, dec_ref, fw_ref, con_ref, sems = refs[-5:]
    _, layers, rows, cols = inc_ref.shape
    copies = fetch([(inc_hbm, inc_ref), (dec_hbm, dec_ref), (fw_hbm, fw_ref), (con_hbm, con_ref)], sems)
    ysend_ref[...] = jnp.zeros(ysend_ref.shape, F32)
    for copy in copies:
        copy.wait()
    product = dec_ref[:, 0, :]
    value = inc_ref[:, 0, 0, :]
    for y in range(1, rows):
        decay = dec_ref[:, y, :]
        product = product * decay
        value = value * decay + inc_ref[:, 0, y, :]
    pair = lax.broadcasted_iota(jnp.int32, (rows, cols), 1) >> 1
    row = lax.broadcasted_iota(jnp.int32, (rows, cols), 0)
    packed = jnp.zeros((rows, cols), F32)
    planes = unknowns * layers
    for p in range(planes):
        packed = jnp.where(pair == p, pltpu.roll(inc_ref[p // layers, p % layers], 2 * p + 1, 1), packed)
    faces = [[fw_ref[d, l] * con_ref[d, l].astype(F32) for l in range(layers)] for d in range(3)]
    for layer in range(layers):
        p = planes + layer
        packed = jnp.where(pair == p, pltpu.roll(faces[0][layer], 2 * p + 1, 1), packed)
    ysend_ref[0, 0:unknowns] = product
    ysend_ref[1, 0:unknowns] = value
    for layer in range(layers):
        ysend_ref[2 + layer, 0:unknowns] = inc_ref[:, layer, 0, :]
        ysend_ref[2 + layers + layer, 0:unknowns] = inc_ref[:, layer, rows - 1, :]
        ysend_ref[2 + layers + layer, unknowns:unknowns + 1] = faces[1][layer][rows - 1:]
        face_out[layer][...] = faces[0][layer]
        face_out[layers + layer][...] = jnp.where(row == rows - 1, 0.0, faces[1][layer])
        face_out[2 * layers + layer][...] = faces[2][layer]
    packed_ref[...] = packed
    for u in range(unknowns):
        inc_out[u][...] = inc_ref[u]


def river_rows(xsend_ref, rows, at, value):
    for c in range(value.shape[1] // LANES):
        xsend_ref[pl.ds(rows + at + c, 1), :] = value[:, c * LANES:(c + 1) * LANES]


def river_kernel(pad, reach_local, code_ref, outflow_ref, inflow_ref, storage_ref, packed_ref, inc_ref, _, xsend_ref):
    layers, rows, cols = inc_ref.shape
    slots = code_ref.shape[2]
    wide = slots // LANES
    code = code_ref[0].astype(jnp.int32)
    reaches = code >> log2(rows * cols)
    cells = code & (rows * cols - 1)
    xsend_ref[rows:, :] = jnp.zeros((xsend_ref.shape[0] - rows, LANES), F32)
    xsend_ref[0:rows, :] = packed_ref[...]
    river_rows(xsend_ref, rows, 2 * pad, cells.astype(F32))
    river_rows(xsend_ref, rows, 2 * pad + wide, reaches.astype(F32))
    river_rows(xsend_ref, rows, 2 * pad + 2 * wide, outflow_ref[0])
    y_hot = hot(cells >> log2(cols), rows).astype(F32)
    y_hot3 = jnp.concatenate([y_hot, y_hot, y_hot], 0).astype(BF16)
    parts = jnp.concatenate(split3(inc_ref[0]), 0).astype(BF16)
    picked = lax.dot_general(parts, y_hot3, (((0,), (0,)), ((), ())), preferred_element_type=F32)
    values = jnp.sum(jnp.where(hot(cells & (cols - 1), cols), picked, 0.0), 0, keepdims=True)
    terms = stack3(inflow_ref[0] * values, 16)
    x_index = lax.axis_index("tx")
    owner = lax.broadcasted_iota(jnp.int32, (1, LANES), 1)
    stored = jnp.concatenate([storage_ref[0, :, 0:reach_local]] * (LANES // reach_local), 1)
    for c in range(reach_local * lax.axis_size("tx") // LANES):
        r_hot = hot(reaches, LANES, c * LANES).astype(F32).astype(BF16)
        total = lax.dot_general(terms, r_hot, (((1,), (1,)), ((), ())), preferred_element_type=F32)
        xsend_ref[pl.ds(rows + c, 1), :] = jnp.sum(total, 0, keepdims=True)
        xsend_ref[pl.ds(rows + pad + c, 1), :] = jnp.where(
            (owner + c * LANES) // reach_local == x_index, stored, 0.0
        )


def prefix_step(k, received, prior):
    upper = bit_of("ty", k) == 1
    if prior is None:
        return jnp.where(upper, received[0], 1.0), jnp.where(upper, received[1], 0.0)
    product = jnp.where(upper, prior[0] * received[0], prior[0])
    value = jnp.where(upper, prior[0] * received[1] + prior[1], prior[1])
    return product, value


def between_kernel(k, layers, sent_ref, got_ref, *refs):
    prior_ref = refs[0] if k > 0 else None
    send_ref, next_ref = refs[-2:]
    upper = bit_of("ty", k) == 1
    product, value = prefix_step(k, got_ref, prior_ref)
    next_ref[0] = product
    next_ref[1] = value
    own_a, own_b, got_a, got_b = sent_ref[0], sent_ref[1], got_ref[0], got_ref[1]
    low_b = jnp.where(upper, got_b, own_b)
    up_a = jnp.where(upper, own_a, got_a)
    up_b = jnp.where(upper, own_b, got_b)
    lead = send_ref.shape[0] - layers
    send_ref[lead - 1] = up_a * low_b + up_b
    if lead == 2:
        send_ref[0] = own_a * got_a
    for layer in range(layers):
        passed = got_ref[2 + layer]
        if k == 0:
            passed = jnp.where(upper, passed, got_ref[2 + layers + layer])
        send_ref[lead + layer] = passed


def sum_kernel(start, stop, sent_ref, got_ref, _, send_ref):
    send_ref[...] = sent_ref[...]
    send_ref[start:stop, :] = sent_ref[start:stop, :] + got_ref[start:stop, :]


def beside_x(received, rows):
    index = lax.axis_index("tx")
    below = jnp.zeros((rows, LANES), F32)
    above = below
    for k, buffer in enumerate(received):
        low = (1 << k) - 1
        full = (2 << k) - 1
        above = jnp.where((index & full) == low, buffer[0:rows, :], above)
        below = jnp.where((index & full) == low + 1, buffer[0:rows, :], below)
    return below, above


def multiply(u, blocks, inc_refs, total):
    for j in range(len(inc_refs)):
        total = total + blocks[j].astype(F32) * inc_refs[j][...]
    return total


def ahead_kernel(unknowns, count, blocks_hbm, dec_hbm, *refs):
    inc_refs, refs = refs[2:2 + unknowns], refs[2 + unknowns:]
    out_refs, refs = refs[:unknowns], refs[unknowns:]
    grown_refs, refs = refs[:unknowns], refs[unknowns:]
    blocks_ref, top_ref, dec_ref, value_ref, product_ref, sems = refs
    _, rows, cols = top_ref.shape
    copies = fetch(
        [(dec_hbm, dec_ref)] + [(blocks_hbm.at[i], blocks_ref.at[i]) for i in range(count)], sems
    )
    for u in range(unknowns):
        top_ref[u] = inc_refs[u][0]
    copies[0].wait()
    product = 0.1 * dec_ref[:, 0, :]
    value = 0.1 * top_ref[:, 0, :]
    product_ref[:, 0, :] = product
    value_ref[:, 0, :] = value
    for y in range(1, rows):
        decay = dec_ref[:, y, :]
        product = product * decay
        value = value * decay + 0.1 * top_ref[:, y, :]
        product_ref[:, y, :] = product
        value_ref[:, y, :] = value
    for u in range(unknowns):
        grown_refs[u][...] = product_ref[u]
        if u >= count:
            out_refs[u][...] = value_ref[u]
            continue
        if u % WAITS == 0:
            for copy in copies[1 + u:1 + min(u + WAITS, count)]:
                copy.wait()
        total = multiply(u, blocks_ref.at[u], inc_refs, jnp.zeros(out_refs[u].shape, F32))
        out_refs[u][0] = total[0] + value_ref[u]
        out_refs[u][1:] = total[1:]


def local_kernel(x_rounds, pad, reach_rows, slots, unknowns, layers, count, blocks_hbm, sent_ref, *refs):
    received, refs = refs[:x_rounds], refs[x_rounds:]
    inc_refs, refs = refs[:unknowns], refs[unknowns:]
    face_refs, refs = refs[:3 * layers], refs[3 * layers:]
    done_refs, refs = refs[:unknowns], refs[unknowns:]
    out_refs, refs = refs[:unknowns], refs[unknowns:]
    blocks_ref, flux_ref, sems = refs
    _, rows, cols = inc_refs[0].shape
    copies = fetch(
        [(blocks_hbm.at[i], blocks_ref.at[i - count]) for i in range(count, unknowns)],
        sems,
    )
    lane = lax.broadcasted_iota(jnp.int32, (rows, cols), 1)
    wide = slots // LANES

    def slot_row(at):
        start = rows + 2 * pad + at * wide
        return jnp.concatenate([sent_ref[start + c:start + c + 1, :] for c in range(wide)], 1)

    cells = slot_row(0).astype(jnp.int32)
    reaches = slot_row(1).astype(jnp.int32)
    totals = sent_ref[rows:rows + pad, :] + received[-1][rows:rows + pad, :]
    storage = sent_ref[rows + pad:rows + 2 * pad, :] + received[-1][rows + pad:rows + 2 * pad, :]
    shift = log2(cols)
    picked = jnp.zeros((16, slots), F32)
    for c in range(reach_rows):
        section = stack3(totals[c:c + 1] / storage[c:c + 1], 16)
        r_hot = hot(reaches, LANES, c * LANES).astype(F32).astype(BF16)
        picked = picked + lax.dot_general(section, r_hot, (((1,), (0,)), ((), ())), preferred_element_type=F32)
    back = slot_row(2) * jnp.sum(picked, 0, keepdims=True)
    y_hot = hot(cells >> shift, rows)
    spread = jnp.concatenate([jnp.where(y_hot, part, 0.0) for part in split3(back)], 0).astype(BF16)
    x_hot = hot(cells & (cols - 1), cols).astype(F32).astype(BF16)
    added = lax.dot_general(spread, x_hot, (((1,), (1,)), ((), ())), preferred_element_type=F32)
    river = added[0:rows] + added[rows:2 * rows] + added[2 * rows:3 * rows]
    left, right = beside_x(received, rows)
    rim = jnp.where(lane & 1 == 0, pltpu.roll(right, cols - 1, 1), pltpu.roll(left, 1, 1))
    planes = unknowns * layers
    for layer in range(layers):
        face_x = face_refs[layer][...]
        face_y = face_refs[layers + layer][...]
        face_z = face_refs[2 * layers + layer][...]
        face_left = pltpu.roll(rim, (cols - 1 - 2 * (planes + layer)) % cols, 1)
        for first in range(0, unknowns, GROUP):
            group = range(first, min(first + GROUP, unknowns))
            here = jnp.stack([inc_refs[u][layer] for u in group])
            beside = jnp.stack([pltpu.roll(rim, cols - 1 - 2 * (u * layers + layer), 1) for u in group])
            flow_x = face_x * (here - jnp.where(lane == cols - 1, beside, pltpu.roll(here, cols - 1, 2)))
            from_left = jnp.where(lane == 0, face_left * (beside - here), pltpu.roll(flow_x, 1, 2))
            flow_y = face_y * (here - pltpu.roll(here, rows - 1, 1))
            total = flow_x - from_left + (flow_y - pltpu.roll(flow_y, 1, 1))
            if layer + 1 < layers:
                total = total + face_z * (here - jnp.stack([inc_refs[u][layer + 1] for u in group]))
            else:
                total = total + face_z * here
            if layer > 0:
                over = jnp.stack([inc_refs[u][layer - 1] for u in group])
                total = total + face_refs[2 * layers + layer - 1][...] * (here - over)
            for u in group:
                flux_ref[u, layer] = total[u - first]
    for u in [*range(1, unknowns), 0]:
        total = flux_ref[u]
        if u < count:
            total = total + done_refs[u][...]
            if u == 0:
                out_refs[u][0] = total[0] + river
                out_refs[u][1:] = total[1:]
            else:
                out_refs[u][...] = total
            continue
        at = u - count
        if at % WAITS == 0:
            for copy in copies[at:at + WAITS]:
                copy.wait()
        total = multiply(u, blocks_ref.at[at], inc_refs, total)
        out_refs[u][0] = total[0] + done_refs[u][...]
        out_refs[u][1:] = total[1:]


def final_kernel(unknowns, y_rounds, *refs):
    part_refs = refs[:unknowns]
    grown_refs = refs[unknowns:2 * unknowns]
    own_ref = refs[2 * unknowns]
    got = refs[2 * unknowns + 1:2 * unknowns + 1 + y_rounds]
    prior_ref, out_ref = refs[-2:]
    layers, rows, cols = part_refs[0].shape
    upper = bit_of("ty", y_rounds - 1) == 1
    carry = jnp.where(upper, prior_ref[0] * got[-1][0] + prior_ref[1], prior_ref[1])
    index = lax.axis_index("ty")
    odd = (index & 1) == 1
    at = lax.broadcasted_iota(jnp.int32, (8, cols), 0)
    starts = []
    ends = []
    for layer in range(layers):
        passed_up = jnp.zeros(carry.shape, F32)
        passed_down = passed_up
        for k in range(1, y_rounds):
            full = (2 << k) - 1
            passed_up = jnp.where((index & full) == (1 << k), got[k][got[k].shape[0] - layers + layer], passed_up)
            passed_down = jnp.where((index & full) == (1 << k) - 1, got[k][got[k].shape[0] - layers + layer], passed_down)
        below = jnp.where(odd, got[0][2 + layers + layer], passed_up)
        above = jnp.where(odd, passed_down, got[0][2 + layer])
        low_face = below[unknowns:unknowns + 1]
        top_face = own_ref[2 + layers + layer, unknowns:unknowns + 1]
        starts.append(low_face * (own_ref[2 + layer] - below))
        ends.append(top_face * (own_ref[2 + layers + layer] - above))
    for u in range(unknowns):
        for layer in range(layers):
            total = part_refs[u][layer]
            if layer == 0:
                total = total + grown_refs[u][...] * carry[u:u + 1]
            head = total[0:8] + jnp.where(at == 0, starts[layer][u:u + 1], 0.0)
            foot = total[rows - 8:rows] + jnp.where(at == 7, ends[layer][u:u + 1], 0.0)
            out_ref[u, layer, 0:8, :] = head
            out_ref[u, layer, 8:rows - 8, :] = total[8:rows - 8]
            out_ref[u, layer, rows - 8:rows, :] = foot


def call(kernel, outs, args, far=0, scratch=(), grant=32 * 1024, cost=0):
    vmem = pl.BlockSpec(memory_space=pltpu.VMEM)
    hbm = pl.BlockSpec(memory_space=pltpu.HBM)
    return pl.pallas_call(
        kernel,
        out_shape=[jax.ShapeDtypeStruct(o.shape, o.dtype) for o in outs],
        in_specs=[hbm] * far + [vmem] * (len(args) - far),
        out_specs=[vmem] * len(outs),
        scratch_shapes=list(scratch),
        compiler_params=pltpu.CompilerParams(vmem_limit_bytes=grant * 1024),
        cost_estimate=pl.CostEstimate(flops=0, bytes_accessed=cost, transcendentals=0),
    )(*args)


def f32(*shape):
    return jax.ShapeDtypeStruct(shape, F32)


def like(a, *shape):
    return pltpu.VMEM(shape or a.shape, a.dtype)


SUMMARY_GRANT = 54600
LOCAL_GRANT = 52000
LOCAL_COST = 0
RIVER_COST = 0
GROUP = 13
WAITS = 2
AHEAD = 5
EXTRA = 0
AHEAD_GRANT = 54180


def body(
    increment,
    blocks,
    face_weights,
    connected,
    overland_decay,
    river_cell,
    river_reach,
    river_count,
    inflow,
    outflow,
    storage,
):
    unknowns, layers, rows, cols = increment.shape
    x_size = lax.axis_size("tx")
    y_size = lax.axis_size("ty")
    x_rounds = log2(x_size)
    y_rounds = log2(y_size)
    slots = river_cell.shape[2]
    decay = jnp.swapaxes(overland_decay, 1, 2)
    reach_rows = storage.shape[1] * x_size // LANES
    pad = -(-reach_rows // 8) * 8
    tall = -(-(unknowns + 1) // 8) * 8
    plane = f32(rows, cols)
    y_first, packed, *kept = call(
        functools.partial(summary_kernel, unknowns),
        [f32(2 + 2 * layers, tall, cols), plane] + [f32(layers, rows, cols)] * unknowns + [plane] * (3 * layers),
        [increment, decay, face_weights, connected],
        far=4,
        scratch=[
            like(increment), like(decay), like(face_weights), like(connected), pltpu.SemaphoreType.DMA((4,)),
        ],
        grant=SUMMARY_GRANT,
    )
    live = lax.broadcasted_iota(jnp.int32, river_cell.shape, 2) < river_count[:, :, None]
    code = jnp.where(live, (river_cell + (rows * cols) * river_reach).astype(F32), 0.0)
    reach_local = storage.shape[1]
    stored = jnp.pad(storage[None], ((0, 0), (0, 0), (0, slots - reach_local)))
    stored = jnp.where(lax.broadcasted_iota(jnp.int32, stored.shape, 2) < reach_local, stored, jnp.where(live, 1.0, 0.0))
    (x_send,) = call(
        functools.partial(river_kernel, pad, reach_local),
        [f32(EXTRA + rows + 2 * pad + -(-3 * slots // LANES // 8) * 8, cols)],
        [code, jnp.where(live, outflow, 0.0), jnp.where(live, inflow, 0.0), stored, packed, kept[0], y_first],
        cost=RIVER_COST,
    )
    y_send = y_first
    y_got = []
    x_got = []
    prior = None
    ahead = (y_first,)
    for k in range(max(x_rounds, y_rounds)):
        if k < y_rounds:
            y_got.append(lax.ppermute(y_send, "ty", [(i, i ^ (1 << k)) for i in range(y_size)]))
        if k < x_rounds:
            x_got.append(lax.ppermute(x_send, "tx", [(i, i ^ ((2 << k) - 1)) for i in range(x_size)]))
        if k + 1 < y_rounds:
            y_send, prior = call(
                functools.partial(between_kernel, k, layers),
                [f32((2 if k + 2 < y_rounds else 1) + layers, tall, cols), f32(2, tall, cols)],
                [y_send, y_got[-1]] + ([prior, x_send] if k > 0 else []),
            )
            if k == 0:
                made = call(
                    functools.partial(ahead_kernel, unknowns, AHEAD),
                    [f32(layers, rows, cols)] * AHEAD + [plane] * (2 * unknowns - AHEAD),
                    [blocks, decay, y_send, y_send, *kept[:unknowns]],
                    far=2,
                    scratch=[
                        like(blocks, AHEAD, *blocks.shape[1:]), like(decay), like(decay), like(decay), like(decay),
                        pltpu.SemaphoreType.DMA((1 + AHEAD,)),
                    ],
                    grant=AHEAD_GRANT,
                )
                ahead, grown = made[:unknowns], made[unknowns:]
        if k + 1 < x_rounds:
            (x_send,) = call(
                functools.partial(sum_kernel, rows, rows + 2 * pad), [x_send], [x_send, x_got[-1], ahead[0]]
            )
    local = call(
        functools.partial(local_kernel, x_rounds, pad, reach_rows, slots, unknowns, layers, AHEAD),
        [f32(layers, rows, cols)] * unknowns,
        [blocks, x_send, *x_got, *kept, *ahead],
        far=1,
        scratch=[
            like(blocks, unknowns - AHEAD, *blocks.shape[1:]), like(increment),
            pltpu.SemaphoreType.DMA((unknowns - AHEAD,)),
        ],
        grant=LOCAL_GRANT,
        cost=LOCAL_COST,
    )
    (total,) = call(
        functools.partial(final_kernel, unknowns, y_rounds),
        [increment],
        [*local, *grown, y_first, *y_got, prior],
    )
    return total


def solution(mesh):
    in_specs = (
        P(None, None, "ty", "tx"),
        P(None, None, None, "ty", "tx"),
        P(None, None, "ty", "tx"),
        P(None, None, "ty", "tx"),
        P(None, "tx", "ty"),
        P("tx", "ty", None),
        P("tx", "ty", None),
        P("tx", "ty"),
        P("tx", "ty", None),
        P("tx", "ty", None),
        P("ty", "tx"),
    )
    out_specs = P(None, None, "ty", "tx")
    return jax.shard_map(body, mesh=mesh, in_specs=in_specs, out_specs=out_specs, check_vma=False)
```

```python
import functools
import jax
import jax.numpy as jnp
from jax import lax
from jax.experimental import pallas as pl
from jax.experimental.pallas import tpu as pltpu
from jax.sharding import PartitionSpec as P

F32 = jnp.float32
BF16 = jnp.bfloat16
LANES = 128


def log2(n):
    return n.bit_length() - 1


def bit_of(axis, k):
    return (lax.axis_index(axis) >> k) & 1


def split3(x):
    hi = x.astype(BF16).astype(F32)
    rest = x - hi
    mid = rest.astype(BF16).astype(F32)
    return hi, mid, rest - mid


def stack3(row, height):
    hi, mid, lo = split3(row)
    at = lax.broadcasted_iota(jnp.int32, (height, row.shape[1]), 0)
    zero = jnp.zeros((height, row.shape[1]), F32)
    out = jnp.where(at == 0, hi, jnp.where(at == 1, mid, jnp.where(at == 2, lo, zero)))
    return out.astype(BF16)


def hot(index_row, size, start=0):
    at = lax.broadcasted_iota(jnp.int32, (size, index_row.shape[1]), 0) + start
    return at == index_row


def fetch(pairs, sems):
    copies = [pltpu.make_async_copy(src, dst, sems.at[i]) for i, (src, dst) in enumerate(pairs)]
    for copy in copies:
        copy.start()
    return copies


def summary_kernel(unknowns, inc_hbm, dec_hbm, fw_hbm, con_hbm, ysend_ref, packed_ref, *refs):
    inc_out = refs[:unknowns]
    face_out = refs[unknowns:-5]
    inc_ref, dec_ref, fw_ref, con_ref, sems = refs[-5:]
    _, layers, rows, cols = inc_ref.shape
    copies = fetch([(inc_hbm, inc_ref), (dec_hbm, dec_ref), (fw_hbm, fw_ref), (con_hbm, con_ref)], sems)
    ysend_ref[...] = jnp.zeros(ysend_ref.shape, F32)
    for copy in copies:
        copy.wait()
    product = dec_ref[:, 0, :]
    value = inc_ref[:, 0, 0, :]
    for y in range(1, rows):
        decay = dec_ref[:, y, :]
        product = product * decay
        value = value * decay + inc_ref[:, 0, y, :]
    pair = lax.broadcasted_iota(jnp.int32, (rows, cols), 1) >> 1
    row = lax.broadcasted_iota(jnp.int32, (rows, cols), 0)
    packed = jnp.zeros((rows, cols), F32)
    planes = unknowns * layers
    for p in range(planes):
        packed = jnp.where(pair == p, pltpu.roll(inc_ref[p // layers, p % layers], 2 * p + 1, 1), packed)
    faces = [[fw_ref[d, l] * con_ref[d, l].astype(F32) for l in range(layers)] for d in range(3)]
    for layer in range(layers):
        p = planes + layer
        packed = jnp.where(pair == p, pltpu.roll(faces[0][layer], 2 * p + 1, 1), packed)
    ysend_ref[0, 0:unknowns] = product
    ysend_ref[1, 0:unknowns] = value
    for layer in range(layers):
        ysend_ref[2 + layer, 0:unknowns] = inc_ref[:, layer, 0, :]
        ysend_ref[2 + layers + layer, 0:unknowns] = inc_ref[:, layer, rows - 1, :]
        ysend_ref[2 + layers + layer, unknowns:unknowns + 1] = faces[1][layer][rows - 1:]
        face_out[layer][...] = faces[0][layer]
        face_out[layers + layer][...] = jnp.where(row == rows - 1, 0.0, faces[1][layer])
        face_out[2 * layers + layer][...] = faces[2][layer]
    packed_ref[...] = packed
    for u in range(unknowns):
        inc_out[u][...] = inc_ref[u]


def river_rows(xsend_ref, rows, at, value):
    for c in range(value.shape[1] // LANES):
        xsend_ref[pl.ds(rows + at + c, 1), :] = value[:, c * LANES:(c + 1) * LANES]


def river_kernel(pad, reach_local, code_ref, outflow_ref, inflow_ref, storage_ref, packed_ref, inc_ref, _, xsend_ref):
    layers, rows, cols = inc_ref.shape
    slots = code_ref.shape[2]
    wide = slots // LANES
    code = code_ref[0].astype(jnp.int32)
    reaches = code >> log2(rows * cols)
    cells = code & (rows * cols - 1)
    xsend_ref[rows:, :] = jnp.zeros((xsend_ref.shape[0] - rows, LANES), F32)
    xsend_ref[0:rows, :] = packed_ref[...]
    river_rows(xsend_ref, rows, 2 * pad, cells.astype(F32))
    river_rows(xsend_ref, rows, 2 * pad + wide, reaches.astype(F32))
    river_rows(xsend_ref, rows, 2 * pad + 2 * wide, outflow_ref[0])
    y_hot = hot(cells >> log2(cols), rows).astype(F32)
    y_hot3 = jnp.concatenate([y_hot, y_hot, y_hot], 0).astype(BF16)
    parts = jnp.concatenate(split3(inc_ref[0]), 0).astype(BF16)
    picked = lax.dot_general(parts, y_hot3, (((0,), (0,)), ((), ())), preferred_element_type=F32)
    values = jnp.sum(jnp.where(hot(cells & (cols - 1), cols), picked, 0.0), 0, keepdims=True)
    terms = stack3(inflow_ref[0] * values, 16)
    x_index = lax.axis_index("tx")
    owner = lax.broadcasted_iota(jnp.int32, (1, LANES), 1)
    stored = jnp.concatenate([storage_ref[0, :, 0:reach_local]] * (LANES // reach_local), 1)
    for c in range(reach_local * lax.axis_size("tx") // LANES):
        r_hot = hot(reaches, LANES, c * LANES).astype(F32).astype(BF16)
        total = lax.dot_general(terms, r_hot, (((1,), (1,)), ((), ())), preferred_element_type=F32)
        xsend_ref[pl.ds(rows + c, 1), :] = jnp.sum(total, 0, keepdims=True)
        xsend_ref[pl.ds(rows + pad + c, 1), :] = jnp.where(
            (owner + c * LANES) // reach_local == x_index, stored, 0.0
        )


def prefix_step(k, received, prior):
    upper = bit_of("ty", k) == 1
    if prior is None:
        return jnp.where(upper, received[0], 1.0), jnp.where(upper, received[1], 0.0)
    product = jnp.where(upper, prior[0] * received[0], prior[0])
    value = jnp.where(upper, prior[0] * received[1] + prior[1], prior[1])
    return product, value


def between_kernel(k, layers, sent_ref, got_ref, *refs):
    prior_ref = refs[0] if k > 0 else None
    send_ref, next_ref = refs[-2:]
    upper = bit_of("ty", k) == 1
    product, value = prefix_step(k, got_ref, prior_ref)
    next_ref[0] = product
    next_ref[1] = value
    own_a, own_b, got_a, got_b = sent_ref[0], sent_ref[1], got_ref[0], got_ref[1]
    low_b = jnp.where(upper, got_b, own_b)
    up_a = jnp.where(upper, own_a, got_a)
    up_b = jnp.where(upper, own_b, got_b)
    lead = send_ref.shape[0] - layers
    send_ref[lead - 1] = up_a * low_b + up_b
    if lead == 2:
        send_ref[0] = own_a * got_a
    for layer in range(layers):
        passed = got_ref[2 + layer]
        if k == 0:
            passed = jnp.where(upper, passed, got_ref[2 + layers + layer])
        send_ref[lead + layer] = passed


def sum_kernel(start, stop, sent_ref, got_ref, _, send_ref):
    send_ref[...] = sent_ref[...]
    send_ref[start:stop, :] = sent_ref[start:stop, :] + got_ref[start:stop, :]


def beside_x(received, rows):
    index = lax.axis_index("tx")
    below = jnp.zeros((rows, LANES), F32)
    above = below
    for k, buffer in enumerate(received):
        low = (1 << k) - 1
        full = (2 << k) - 1
        above = jnp.where((index & full) == low, buffer[0:rows, :], above)
        below = jnp.where((index & full) == low + 1, buffer[0:rows, :], below)
    return below, above


def multiply(u, blocks, inc_refs, total):
    for j in range(len(inc_refs)):
        total = total + blocks[j].astype(F32) * inc_refs[j][...]
    return total


def ahead_kernel(unknowns, count, blocks_hbm, dec_hbm, *refs):
    inc_refs, refs = refs[2:2 + unknowns], refs[2 + unknowns:]
    out_refs, refs = refs[:unknowns], refs[unknowns:]
    grown_refs, refs = refs[:unknowns], refs[unknowns:]
    blocks_ref, top_ref, dec_ref, value_ref, product_ref, sems = refs
    _, rows, cols = top_ref.shape
    copies = fetch(
        [(dec_hbm, dec_ref)] + [(blocks_hbm.at[i], blocks_ref.at[i]) for i in range(count)], sems
    )
    for u in range(unknowns):
        top_ref[u] = inc_refs[u][0]
    copies[0].wait()
    product = 0.1 * dec_ref[:, 0, :]
    value = 0.1 * top_ref[:, 0, :]
    product_ref[:, 0, :] = product
    value_ref[:, 0, :] = value
    for y in range(1, rows):
        decay = dec_ref[:, y, :]
        product = product * decay
        value = value * decay + 0.1 * top_ref[:, y, :]
        product_ref[:, y, :] = product
        value_ref[:, y, :] = value
    for u in range(unknowns):
        grown_refs[u][...] = product_ref[u]
        if u >= count:
            out_refs[u][...] = value_ref[u]
            continue
        if u % WAITS == 0:
            for copy in copies[1 + u:1 + min(u + WAITS, count)]:
                copy.wait()
        total = multiply(u, blocks_ref.at[u], inc_refs, jnp.zeros(out_refs[u].shape, F32))
        out_refs[u][0] = total[0] + value_ref[u]
        out_refs[u][1:] = total[1:]


def local_kernel(x_rounds, pad, reach_rows, slots, unknowns, layers, count, blocks_hbm, sent_ref, *refs):
    received, refs = refs[:x_rounds], refs[x_rounds:]
    inc_refs, refs = refs[:unknowns], refs[unknowns:]
    face_refs, refs = refs[:3 * layers], refs[3 * layers:]
    done_refs, refs = refs[:unknowns], refs[unknowns:]
    out_refs, refs = refs[:unknowns], refs[unknowns:]
    blocks_ref, flux_ref, sems = refs
    _, rows, cols = inc_refs[0].shape
    copies = fetch(
        [(blocks_hbm.at[i], blocks_ref.at[i - count]) for i in range(count, unknowns)],
        sems,
    )
    lane = lax.broadcasted_iota(jnp.int32, (rows, cols), 1)
    wide = slots // LANES

    def slot_row(at):
        start = rows + 2 * pad + at * wide
        return jnp.concatenate([sent_ref[start + c:start + c + 1, :] for c in range(wide)], 1)

    cells = slot_row(0).astype(jnp.int32)
    reaches = slot_row(1).astype(jnp.int32)
    totals = sent_ref[rows:rows + pad, :] + received[-1][rows:rows + pad, :]
    storage = sent_ref[rows + pad:rows + 2 * pad, :] + received[-1][rows + pad:rows + 2 * pad, :]
    shift = log2(cols)
    picked = jnp.zeros((16, slots), F32)
    for c in range(reach_rows):
        section = stack3(totals[c:c + 1] / storage[c:c + 1], 16)
        r_hot = hot(reaches, LANES, c * LANES).astype(F32).astype(BF16)
        picked = picked + lax.dot_general(section, r_hot, (((1,), (0,)), ((), ())), preferred_element_type=F32)
    back = slot_row(2) * jnp.sum(picked, 0, keepdims=True)
    y_hot = hot(cells >> shift, rows)
    spread = jnp.concatenate([jnp.where(y_hot, part, 0.0) for part in split3(back)], 0).astype(BF16)
    x_hot = hot(cells & (cols - 1), cols).astype(F32).astype(BF16)
    added = lax.dot_general(spread, x_hot, (((1,), (1,)), ((), ())), preferred_element_type=F32)
    river = added[0:rows] + added[rows:2 * rows] + added[2 * rows:3 * rows]
    left, right = beside_x(received, rows)
    rim = jnp.where(lane & 1 == 0, pltpu.roll(right, cols - 1, 1), pltpu.roll(left, 1, 1))
    planes = unknowns * layers
    for layer in range(layers):
        face_x = face_refs[layer][...]
        face_y = face_refs[layers + layer][...]
        face_z = face_refs[2 * layers + layer][...]
        face_left = pltpu.roll(rim, (cols - 1 - 2 * (planes + layer)) % cols, 1)
        for first in range(0, unknowns, GROUP):
            group = range(first, min(first + GROUP, unknowns))
            here = jnp.stack([inc_refs[u][layer] for u in group])
            beside = jnp.stack([pltpu.roll(rim, cols - 1 - 2 * (u * layers + layer), 1) for u in group])
            flow_x = face_x * (here - jnp.where(lane == cols - 1, beside, pltpu.roll(here, cols - 1, 2)))
            from_left = jnp.where(lane == 0, face_left * (beside - here), pltpu.roll(flow_x, 1, 2))
            flow_y = face_y * (here - pltpu.roll(here, rows - 1, 1))
            total = flow_x - from_left + (flow_y - pltpu.roll(flow_y, 1, 1))
            if layer + 1 < layers:
                total = total + face_z * (here - jnp.stack([inc_refs[u][layer + 1] for u in group]))
            else:
                total = total + face_z * here
            if layer > 0:
                over = jnp.stack([inc_refs[u][layer - 1] for u in group])
                total = total + face_refs[2 * layers + layer - 1][...] * (here - over)
            for u in group:
                flux_ref[u, layer] = total[u - first]
    for u in [*range(1, unknowns), 0]:
        total = flux_ref[u]
        if u < count:
            total = total + done_refs[u][...]
            if u == 0:
                out_refs[u][0] = total[0] + river
                out_refs[u][1:] = total[1:]
            else:
                out_refs[u][...] = total
            continue
        at = u - count
        if at % WAITS == 0:
            for copy in copies[at:at + WAITS]:
                copy.wait()
        total = multiply(u, blocks_ref.at[at], inc_refs, total)
        out_refs[u][0] = total[0] + done_refs[u][...]
        out_refs[u][1:] = total[1:]


def final_kernel(unknowns, y_rounds, *refs):
    part_refs = refs[:unknowns]
    grown_refs = refs[unknowns:2 * unknowns]
    own_ref = refs[2 * unknowns]
    got = refs[2 * unknowns + 1:2 * unknowns + 1 + y_rounds]
    prior_ref, out_ref = refs[-2:]
    layers, rows, cols = part_refs[0].shape
    upper = bit_of("ty", y_rounds - 1) == 1
    carry = jnp.where(upper, prior_ref[0] * got[-1][0] + prior_ref[1], prior_ref[1])
    index = lax.axis_index("ty")
    odd = (index & 1) == 1
    at = lax.broadcasted_iota(jnp.int32, (8, cols), 0)
    starts = []
    ends = []
    for layer in range(layers):
        passed_up = jnp.zeros(carry.shape, F32)
        passed_down = passed_up
        for k in range(1, y_rounds):
            full = (2 << k) - 1
            passed_up = jnp.where((index & full) == (1 << k), got[k][got[k].shape[0] - layers + layer], passed_up)
            passed_down = jnp.where((index & full) == (1 << k) - 1, got[k][got[k].shape[0] - layers + layer], passed_down)
        below = jnp.where(odd, got[0][2 + layers + layer], passed_up)
        above = jnp.where(odd, passed_down, got[0][2 + layer])
        low_face = below[unknowns:unknowns + 1]
        top_face = own_ref[2 + layers + layer, unknowns:unknowns + 1]
        starts.append(low_face * (own_ref[2 + layer] - below))
        ends.append(top_face * (own_ref[2 + layers + layer] - above))
    for u in range(unknowns):
        for layer in range(layers):
            total = part_refs[u][layer]
            if layer == 0:
                total = total + grown_refs[u][...] * carry[u:u + 1]
            head = total[0:8] + jnp.where(at == 0, starts[layer][u:u + 1], 0.0)
            foot = total[rows - 8:rows] + jnp.where(at == 7, ends[layer][u:u + 1], 0.0)
            out_ref[u, layer, 0:8, :] = head
            out_ref[u, layer, 8:rows - 8, :] = total[8:rows - 8]
            out_ref[u, layer, rows - 8:rows, :] = foot


def call(kernel, outs, args, far=0, scratch=(), grant=32 * 1024, cost=0):
    vmem = pl.BlockSpec(memory_space=pltpu.VMEM)
    hbm = pl.BlockSpec(memory_space=pltpu.HBM)
    return pl.pallas_call(
        kernel,
        out_shape=[jax.ShapeDtypeStruct(o.shape, o.dtype) for o in outs],
        in_specs=[hbm] * far + [vmem] * (len(args) - far),
        out_specs=[vmem] * len(outs),
        scratch_shapes=list(scratch),
        compiler_params=pltpu.CompilerParams(vmem_limit_bytes=grant * 1024),
        cost_estimate=pl.CostEstimate(flops=0, bytes_accessed=cost, transcendentals=0),
    )(*args)


def f32(*shape):
    return jax.ShapeDtypeStruct(shape, F32)


def like(a, *shape):
    return pltpu.VMEM(shape or a.shape, a.dtype)


SUMMARY_GRANT = 54600
LOCAL_GRANT = 52000
LOCAL_COST = 0
RIVER_COST = 0
GROUP = 13
WAITS = 3
AHEAD = 3
EXTRA = 0
AHEAD_GRANT = 54180


def body(
    increment,
    blocks,
    face_weights,
    connected,
    overland_decay,
    river_cell,
    river_reach,
    river_count,
    inflow,
    outflow,
    storage,
):
    unknowns, layers, rows, cols = increment.shape
    x_size = lax.axis_size("tx")
    y_size = lax.axis_size("ty")
    x_rounds = log2(x_size)
    y_rounds = log2(y_size)
    slots = river_cell.shape[2]
    decay = jnp.swapaxes(overland_decay, 1, 2)
    reach_rows = storage.shape[1] * x_size // LANES
    pad = -(-reach_rows // 8) * 8
    tall = -(-(unknowns + 1) // 8) * 8
    plane = f32(rows, cols)
    y_first, packed, *kept = call(
        functools.partial(summary_kernel, unknowns),
        [f32(2 + 2 * layers, tall, cols), plane] + [f32(layers, rows, cols)] * unknowns + [plane] * (3 * layers),
        [increment, decay, face_weights, connected],
        far=4,
        scratch=[
            like(increment), like(decay), like(face_weights), like(connected), pltpu.SemaphoreType.DMA((4,)),
        ],
        grant=SUMMARY_GRANT,
    )
    live = lax.broadcasted_iota(jnp.int32, river_cell.shape, 2) < river_count[:, :, None]
    code = jnp.where(live, (river_cell + (rows * cols) * river_reach).astype(F32), 0.0)
    reach_local = storage.shape[1]
    stored = jnp.pad(storage[None], ((0, 0), (0, 0), (0, slots - reach_local)))
    stored = jnp.where(lax.broadcasted_iota(jnp.int32, stored.shape, 2) < reach_local, stored, jnp.where(live, 1.0, 0.0))
    (x_send,) = call(
        functools.partial(river_kernel, pad, reach_local),
        [f32(EXTRA + rows + 2 * pad + -(-3 * slots // LANES // 8) * 8, cols)],
        [code, jnp.where(live, outflow, 0.0), jnp.where(live, inflow, 0.0), stored, packed, kept[0], y_first],
        cost=RIVER_COST,
    )
    y_send = y_first
    y_got = []
    x_got = []
    prior = None
    ahead = (y_first,)
    for k in range(max(x_rounds, y_rounds)):
        if k < y_rounds:
            y_got.append(lax.ppermute(y_send, "ty", [(i, i ^ (1 << k)) for i in range(y_size)]))
        if k < x_rounds:
            x_got.append(lax.ppermute(x_send, "tx", [(i, i ^ ((2 << k) - 1)) for i in range(x_size)]))
        if k + 1 < y_rounds:
            y_send, prior = call(
                functools.partial(between_kernel, k, layers),
                [f32((2 if k + 2 < y_rounds else 1) + layers, tall, cols), f32(2, tall, cols)],
                [y_send, y_got[-1]] + ([prior, x_send] if k > 0 else []),
            )
            if k == 0:
                made = call(
                    functools.partial(ahead_kernel, unknowns, AHEAD),
                    [f32(layers, rows, cols)] * AHEAD + [plane] * (2 * unknowns - AHEAD),
                    [blocks, decay, y_send, y_send, *kept[:unknowns]],
                    far=2,
                    scratch=[
                        like(blocks, AHEAD, *blocks.shape[1:]), like(decay), like(decay), like(decay), like(decay),
                        pltpu.SemaphoreType.DMA((1 + AHEAD,)),
                    ],
                    grant=AHEAD_GRANT,
                )
                ahead, grown = made[:unknowns], made[unknowns:]
        if k + 1 < x_rounds:
            (x_send,) = call(
                functools.partial(sum_kernel, rows, rows + 2 * pad), [x_send], [x_send, x_got[-1], ahead[0]]
            )
    local = call(
        functools.partial(local_kernel, x_rounds, pad, reach_rows, slots, unknowns, layers, AHEAD),
        [f32(layers, rows, cols)] * unknowns,
        [blocks, x_send, *x_got, *kept, *ahead],
        far=1,
        scratch=[
            like(blocks, unknowns - AHEAD, *blocks.shape[1:]), like(increment),
            pltpu.SemaphoreType.DMA((unknowns - AHEAD,)),
        ],
        grant=LOCAL_GRANT,
        cost=LOCAL_COST,
    )
    (total,) = call(
        functools.partial(final_kernel, unknowns, y_rounds),
        [increment],
        [*local, *grown, y_first, *y_got, prior],
    )
    return total


def solution(mesh):
    in_specs = (
        P(None, None, "ty", "tx"),
        P(None, None, None, "ty", "tx"),
        P(None, None, "ty", "tx"),
        P(None, None, "ty", "tx"),
        P(None, "tx", "ty"),
        P("tx", "ty", None),
        P("tx", "ty", None),
        P("tx", "ty"),
        P("tx", "ty", None),
        P("tx", "ty", None),
        P("ty", "tx"),
    )
    out_specs = P(None, None, "ty", "tx")
    return jax.shard_map(body, mesh=mesh, in_specs=in_specs, out_specs=out_specs, check_vma=False)
```
